32 devices in a mesh: queue: 8 (over z, y), head: 4 (over x, core).
Axes of the slice: x: 2, y: 2, z: 4, core: 2. Of those that a mesh axis runs over, the one named last changes fastest.
Arguments:
- latents: bfloat16 [1536, 1536], P('queue', 'head'), may hold values from -6 to 6
- fresh_frame: bfloat16 [384, 1536], P(None, 'head'), may hold values from -6 to 6
- noise_level: int32 [4], replicated, may hold values from 0 to 15, as said below
- offset: int32 [1], replicated, may hold values from 0 to 16383
- mod_table: float32 [16, 3, 1536], replicated, may hold values from -4 to 4
- w_qkv: bfloat16 [1536, 3, 1536], P(None, None, 'head'), may hold values from -1 to 1
- w_out: bfloat16 [1536, 1536], P('head'), may hold values from -0.15625 to 0.15625
- q_gain: float32 [1536], P('head'), may hold values from 1 to 3
- k_gain: float32 [1536], P('head'), may hold values from 1 to 3
Outputs:
- advanced: bfloat16 [1536, 1536], P('queue', 'head')
The draws below stay inside these ranges and needn't reach their ends.
Inputs may be any that keep to these rules, and one draw needn't show every extreme that they name: `noise_level`: entry p lies in p * 4 to (p + 1) * 4 - 1.
All inputs are finite; a program needn't handle non-finite values.
Results may differ from the reference program's by a relative error of at most 0.011.
Values may be sent and summed in bfloat16 or wider, within the bound.
A program may use at most 128 MiB of HBM per device.

```python
import math
import jax
import jax.numpy as jnp
from jax import lax

D = 1536
HEADS = 12
DH = 128
TOK_DEV = 192
NOISE_STEP = 4
FRAMES = 4
FRAME_TOK = 384
TOKENS = 1536
LEVELS = 16


def draw_noise_level(key, part):
    key = jax.random.fold_in(key, 7)
    extra = jax.random.randint(key, (FRAMES,), 0, NOISE_STEP)
    index = jnp.arange(FRAMES, dtype=jnp.int32)
    extra = jnp.where(index == 0, 0, extra)
    extra = jnp.where(index == FRAMES - 1, NOISE_STEP - 1, extra)
    return (index * NOISE_STEP + extra).astype(jnp.int32)


def draw_w_qkv(key, part):
    key = jax.random.fold_in(key, 11)
    base_key = jax.random.fold_in(key, 0)
    weights = jnp.clip(jax.random.normal(base_key, (D, 3, D), jnp.float32), -4.0, 4.0) * D ** (-0.5)
    return jnp.clip(weights, -1.0, 1.0).astype(jnp.bfloat16)


def level_of(rng, shape, cuts, least, top_value):
    def one(dim, shards_of):
        steps = jax.random.uniform(jax.random.fold_in(jax.random.fold_in(rng, 6), dim), (shards_of,), jnp.float32, least / len(cuts), top_value / len(cuts))
        return jnp.repeat(jnp.exp(steps), shape[dim] // shards_of).reshape((-1,) + (1,) * (len(shape) - dim - 1))

    factor_of = one(*cuts[0])
    for cut in cuts[1:]:
        factor_of = factor_of * one(*cut)
    return factor_of


def scatter_about(own_key, shape, width, bound, cuts=(), kind=jnp.bfloat16):
    factor_of = level_of(own_key, shape, cuts, -0.22, 0.18) if cuts else 1.0
    entries = jax.random.normal(own_key, shape, jnp.float32) * width * factor_of
    return jnp.minimum(jnp.maximum(entries, -bound), bound).astype(kind)


def setup_inputs(seed: int = 0) -> dict:
    streams_of = jax.random.split(jax.random.key(seed), 10)
    latents = scatter_about(streams_of[0], (TOKENS, D), 1.0, 6.0, ((0, 8), (1, 4)))
    fresh_frame = scatter_about(streams_of[1], (FRAME_TOK, D), 1.0, 6.0, ((1, 4),))
    noise_level = draw_noise_level(jax.random.fold_in(streams_of[9], 71), 0)
    offset = jax.random.randint(streams_of[3], (1,), 0, FRAMES * 4096).astype(jnp.int32)
    mod_table = scatter_about(streams_of[4], (LEVELS, 3, D), 0.6, 4.0, (), jnp.float32)
    w_qkv = draw_w_qkv(jax.random.fold_in(streams_of[9], 71), 0)
    w_out = scatter_about(streams_of[6], (D, D), D ** -0.5, 0.15625, ((0, 4),))
    q_gain = jnp.clip(jnp.exp(math.log(3.0) - 1.0986123 * jax.random.uniform(streams_of[7], (D,), jnp.float32) ** level_of(streams_of[7], (D,), ((0, 4),), -0.2, 0.2)), 1.0, 3.0)
    k_gain = jnp.clip(jnp.exp(math.log(3.0) - 1.0986123 * jax.random.uniform(streams_of[8], (D,), jnp.float32) ** level_of(streams_of[8], (D,), ((0, 4),), -0.2, 0.2)), 1.0, 3.0)
    return {"latents": latents, "fresh_frame": fresh_frame, "noise_level": noise_level, "offset": offset, "mod_table": mod_table, "w_qkv": w_qkv, "w_out": w_out, "q_gain": q_gain, "k_gain": k_gain}


def reference(latents, fresh_frame, noise_level, offset, mod_table, w_qkv, w_out, q_gain, k_gain):
    slots = jnp.arange(FRAMES, dtype=jnp.int32)
    position = jnp.mod(slots - offset[0], FRAMES).astype(jnp.int32)
    levels = noise_level[position]
    modulation = mod_table[levels]
    whole = latents.astype(jnp.float32).reshape(FRAMES, FRAME_TOK, D)
    centered = whole - lax.optimization_barrier(jnp.mean(whole, axis=2, keepdims=True))
    variance = lax.optimization_barrier(jnp.mean(centered * centered, axis=2, keepdims=True))
    normed = centered * lax.rsqrt(variance + 1e-06)
    modded = (normed * (1.0 + modulation[:, 1][:, None, :]) + modulation[:, 0][:, None, :]).astype(jnp.bfloat16)
    modded = modded.reshape(TOKENS, D)
    projected = jnp.dot(modded, w_qkv.reshape(D, 3 * D), preferred_element_type=jnp.float32).reshape(TOKENS, 3, D)
    query_raw = projected[:, 0]
    key_raw = projected[:, 1]
    values = projected[:, 2].astype(jnp.bfloat16)
    queries = (query_raw * lax.rsqrt(lax.optimization_barrier(jnp.mean(query_raw * query_raw, axis=1, keepdims=True)) + 1e-06) * q_gain).astype(jnp.bfloat16)
    key_normed = (key_raw * lax.rsqrt(lax.optimization_barrier(jnp.mean(key_raw * key_raw, axis=1, keepdims=True)) + 1e-06) * k_gain).astype(jnp.bfloat16)
    query_blocks = queries.reshape(2 * FRAMES, TOK_DEV, HEADS, DH)
    block_position = jnp.repeat(position, 2)
    key_heads = key_normed.astype(jnp.float32).reshape(TOKENS, HEADS, DH)
    value_heads = values.astype(jnp.float32).reshape(TOKENS, HEADS, DH)
    key_position = jnp.repeat(position, FRAME_TOK)

    def one_block(operands):
        query_block, query_pos = operands
        scores = jnp.einsum('qhd,khd->hqk', query_block.astype(jnp.float32), key_heads) * DH ** (-0.5)
        allowed = key_position <= query_pos
        scores = jnp.where(allowed[None, None, :], scores, -jnp.inf)
        top_score = lax.optimization_barrier(jnp.max(scores, axis=2, keepdims=True))
        exp_scores = jnp.exp(scores - top_score)
        total = lax.optimization_barrier(jnp.sum(exp_scores, axis=2))
        rounded = lax.optimization_barrier(exp_scores.astype(jnp.bfloat16)).astype(jnp.float32)
        numer = jnp.einsum('hqk,khd->hqd', rounded, value_heads)
        result = numer / total[:, :, None]
        return jnp.transpose(result, (1, 0, 2)).reshape(TOK_DEV, D).astype(jnp.bfloat16)
    attn = lax.map(one_block, (query_blocks, block_position)).reshape(TOKENS, D)
    proj = jnp.dot(attn, w_out, preferred_element_type=jnp.float32).reshape(FRAMES, FRAME_TOK, D)
    updated = (whole + modulation[:, 2][:, None, :] * proj).astype(jnp.bfloat16)
    moved = jnp.roll(updated, -1, axis=0)
    fresh_slot = jnp.mod(offset[0] - 1, FRAMES)
    advanced = jnp.where((slots == fresh_slot)[:, None, None], fresh_frame[None, :, :], moved)
    return advanced.reshape(TOKENS, D)
```

```python
import jax
import jax.numpy as jnp
from jax import lax
from jax.experimental import pallas as pl
from jax.experimental.pallas import tpu as pltpu
from jax.sharding import PartitionSpec as P

D = 1536
DH = 128


def passed_along(block, axis, distance):
    devices = range(lax.axis_size(axis))
    route = [((i - distance) % len(devices), i) for i in devices]
    return lax.ppermute(block, axis, route)


def attend(carried, queries, key_block, value_block, allowed):
    run_max, run_total, running = carried
    key_count = key_block.shape[0]
    head_count = queries.shape[1]
    key_heads = key_block.reshape(key_count, head_count, DH)
    value_heads = value_block.reshape(key_count, head_count, DH)
    scores = jnp.einsum(
        "qhd,khd->hqk", queries, key_heads, preferred_element_type=jnp.float32
    ) * DH ** (-0.5)
    scores = jnp.where(allowed[None, None, :], scores, -jnp.inf)
    new_max = jnp.maximum(run_max, jnp.max(scores, axis=2))
    rescale = jnp.exp(run_max - new_max)
    exp_scores = jnp.exp(scores - new_max[:, :, None])
    new_total = run_total * rescale + jnp.sum(exp_scores, axis=2)
    added = jnp.einsum(
        "hqk,khd->hqd",
        exp_scores.astype(jnp.bfloat16),
        value_heads,
        preferred_element_type=jnp.float32,
    )
    return (new_max, new_total, running * rescale[:, :, None] + added)


def local(latents, fresh_frame, noise_level, offset, mod_table, w_qkv, w_out, q_gain, k_gain):
    slabs = lax.axis_size("queue")
    frames = slabs // 2
    my_slab = lax.axis_index("queue")
    my_frame = my_slab // 2
    position = jnp.mod(my_frame - offset[0], frames)
    my_level = noise_level[position]
    modulation = lax.dynamic_index_in_dim(mod_table, my_level, 0, keepdims=False)
    whole = lax.all_gather(latents, "head", axis=1, tiled=True).astype(jnp.float32)
    row_count = whole.shape[0]
    centered = whole - jnp.mean(whole, axis=1, keepdims=True)
    variance = jnp.mean(centered * centered, axis=1, keepdims=True)
    normed = centered * lax.rsqrt(variance + 1e-06)
    modded = (normed * (1.0 + modulation[1]) + modulation[0]).astype(jnp.bfloat16)
    local_width = w_qkv.shape[2]
    projected = jnp.dot(
        modded, w_qkv.reshape(w_qkv.shape[0], 3 * local_width), preferred_element_type=jnp.float32
    )
    projected = projected.reshape(row_count, 3, local_width)
    query_raw = projected[:, 0]
    key_raw = projected[:, 1]
    values = projected[:, 2].astype(jnp.bfloat16)
    query_sq, key_sq = lax.psum(
        (jnp.sum(query_raw * query_raw, axis=1), jnp.sum(key_raw * key_raw, axis=1)), "head"
    )
    queries = (query_raw * lax.rsqrt(query_sq / D + 1e-06)[:, None] * q_gain).astype(jnp.bfloat16)
    key_normed = (key_raw * lax.rsqrt(key_sq / D + 1e-06)[:, None] * k_gain).astype(jnp.bfloat16)
    head_count = local_width // DH
    query_heads = queries.reshape(row_count, head_count, DH)
    start_state = (
        jnp.full((head_count, row_count), -1e30, jnp.float32),
        jnp.zeros((head_count, row_count), jnp.float32),
        jnp.zeros((head_count, row_count, DH), jnp.float32),
    )
    all_rows = jnp.ones((row_count,), dtype=bool)
    carried = attend(start_state, query_heads, key_normed, values, all_rows)
    stacked = jnp.stack((key_normed, values))

    def pass_step(turn, loop_state):
        pieces, state_now = loop_state
        pieces = passed_along(pieces, "queue", 1)
        key_slab = jnp.mod(my_slab - turn, slabs)
        key_pos = jnp.mod(key_slab // 2 - offset[0], frames)

        def use_piece(state_in):
            return attend(state_in, query_heads, pieces[0], pieces[1], all_rows)

        def keep_state(state_in):
            return state_in

        state_now = lax.cond(key_pos <= position, use_piece, keep_state, state_now)
        return (pieces, state_now)

    stacked, carried = lax.fori_loop(1, slabs, pass_step, (stacked, carried))
    run_max, run_total, running = carried
    attn = (
        jnp.transpose(running / run_total[:, :, None], (1, 0, 2))
        .reshape(row_count, local_width)
        .astype(jnp.bfloat16)
    )
    partial_out = jnp.dot(attn, w_out, preferred_element_type=jnp.float32)
    proj = lax.psum_scatter(
        partial_out.astype(jnp.bfloat16), "head", scatter_dimension=1, tiled=True
    ).astype(jnp.float32)
    feature_start = lax.axis_index("head") * local_width
    gate_local = lax.dynamic_slice_in_dim(modulation[2], feature_start, local_width)
    updated = (latents.astype(jnp.float32) + gate_local * proj).astype(jnp.bfloat16)
    moved = passed_along(updated, "queue", -2)
    entry_slot = jnp.mod(offset[0] - 1, frames)
    fresh_half = lax.dynamic_slice_in_dim(fresh_frame, my_slab % 2 * row_count, row_count, 0)
    return jnp.where(my_frame == entry_slot, fresh_half, moved)


MESH = pl.DeviceIdType.MESH
ZS = 4
ROWS = 192
WIDTH = 384
HEADS_DEV = 3


def arrived(buffer, sem):
    pltpu.make_async_copy(buffer, buffer, sem).wait()


def block_kernel(
    noise_ref, offset_ref, lat_ref, gain_ref, w_hbm, wout_hbm, mod_hbm, out_ref,
    w_v, wo_v, mod_v, lat_buf, mod_act, raw, stat_buf, stage, q_buf, k_buf, v_buf,
    o_buf, a_buf, p_send, rs_buf, upd, fin,
    load_sem, lat_send, lat_recv, st_send, st_recv, qkv_send, q_recv, k_recv, v_recv,
    f_send, o_send, o_recv, rs_send, rs_recv, mv_send, mv_recv,
):
    queue = lax.axis_index("queue")
    head = lax.axis_index("head")
    z, y = queue // 2, queue % 2
    x, c = head // 2, head % 2
    sib = x * 2 + (1 - c)
    xnb = (1 - x) * 2 + c
    diag = (1 - x) * 2 + (1 - c)
    peers = (head, sib, xnb, diag)
    below = queue - 2 + jnp.where(z == 0, 2 * ZS, 0)
    above = queue + 2 - jnp.where(z == ZS - 1, 2 * ZS, 0)
    swap_head = x * 2 + y
    on_diagonal = y == c

    def is_self(zt):
        return jnp.logical_and(on_diagonal, zt == z)

    loads = [
        pltpu.make_async_copy(mod_hbm, mod_v, load_sem.at[0]),
        pltpu.make_async_copy(w_hbm, w_v, load_sem.at[1]),
        pltpu.make_async_copy(wout_hbm, wo_v, load_sem.at[2]),
    ]
    for load in loads:
        load.start()

    barrier = pltpu.get_barrier_semaphore()

    def greet(q_id, h_id):
        pl.semaphore_signal(barrier, inc=1, device_id=(q_id, h_id), device_id_type=MESH)

    for peer in peers[1:]:
        greet(queue, peer)
    greet(below, head)
    greet(above, head)
    for zt in range(ZS):
        pl.when(jnp.logical_not(is_self(zt)))(lambda zt=zt: greet(zt * 2 + c, swap_head))
    pl.semaphore_wait(barrier, 5 + ZS - jnp.where(on_diagonal, 1, 0))

    def remote(src, dst, s_sem, r_sem, q_id, h_id):
        return pltpu.make_async_remote_copy(
            src_ref=src, dst_ref=dst, send_sem=s_sem, recv_sem=r_sem,
            device_id=(q_id, h_id), device_id_type=MESH,
        )

    to_x = remote(lat_ref, lat_buf.at[2], lat_send.at[0], lat_recv.at[2], queue, xnb)
    to_sib = remote(lat_ref, lat_buf.at[1], lat_send.at[1], lat_recv.at[1], queue, sib)
    to_x.start()
    to_sib.start()
    forward = remote(lat_buf.at[2], lat_buf.at[3], lat_send.at[2], lat_recv.at[3], queue, sib)
    arrived(lat_buf.at[2], lat_recv.at[2])
    forward.start()
    arrived(lat_buf.at[1], lat_recv.at[1])
    loads[0].wait()

    offset = lax.rem(offset_ref[0], ZS)

    def position_of(frame):
        return lax.rem(frame + ZS - offset, ZS)

    level = noise_ref[position_of(z)]
    arrived(lat_buf.at[3], lat_recv.at[3])

    def block(r):
        return (lat_ref[...] if r == 0 else lat_buf[r]).astype(jnp.float32)

    def columns(r):
        return pl.ds(pl.multiple_of(peers[r] * WIDTH, WIDTH), WIDTH)

    mean = sum(jnp.sum(block(r), axis=1, keepdims=True) for r in range(4)) / D
    square = jnp.zeros((ROWS, 1), jnp.float32)
    for r in range(4):
        centered = block(r) - mean
        square += jnp.sum(centered * centered, axis=1, keepdims=True)
    inv = lax.rsqrt(square / D + 1e-06)
    for r in range(4):
        shift = mod_v[0, pl.ds(level, 1), columns(r)]
        scale = mod_v[1, pl.ds(level, 1), columns(r)]
        normed = (block(r) - mean) * inv
        mod_act[:, columns(r)] = (normed * (1.0 + scale) + shift).astype(jnp.bfloat16)

    loads[1].wait()
    sums = []
    for i in range(2):
        projected = jnp.dot(mod_act[...], w_v[i], preferred_element_type=jnp.float32)
        raw[i] = projected
        sums.append(jnp.sum(projected * projected, axis=1, keepdims=True))
    lane = lax.broadcasted_iota(jnp.int32, (256, 128), 1)
    padding = jnp.zeros((256 - ROWS, 1), jnp.float32)
    spread = jnp.where(
        lane == 0,
        jnp.concatenate([sums[0], padding], axis=0),
        jnp.concatenate([sums[1], padding], axis=0),
    )
    stat_buf[0] = jnp.transpose(spread)[:8]
    stats = [
        remote(stat_buf.at[0], stat_buf.at[r], st_send.at[r], st_recv.at[r], queue, peers[r])
        for r in (2, 3, 1)
    ]
    for copy in stats:
        copy.start()

    sends = []

    def send_part(part, buf, recv_sem):
        for j in range(HEADS_DEV):
            zt = j + c
            mine = is_self(zt)
            src = stage.at[part, j]
            dst = buf.at[z] if part == 0 else buf.at[0, z]
            far = remote(src, dst, qkv_send.at[part, j], recv_sem.at[z], zt * 2 + c, swap_head)
            near = pltpu.make_async_copy(src, dst, recv_sem.at[z])
            pl.when(mine)(near.start)
            pl.when(jnp.logical_not(mine))(far.start)
            sends.append((mine, far))

    values = jnp.dot(mod_act[...], w_v[2], preferred_element_type=jnp.float32)
    for j in range(HEADS_DEV):
        stage[2, j] = values[:, j * DH:(j + 1) * DH].astype(jnp.bfloat16)
    send_part(2, v_buf, v_recv)

    for r in (1, 2, 3):
        arrived(stat_buf.at[r], st_recv.at[r])
    total_sq = stat_buf[0] + stat_buf[1] + stat_buf[2] + stat_buf[3]
    rates = lax.rsqrt(total_sq / D + 1e-06)
    rates = jnp.transpose(jnp.concatenate([rates] * 16, axis=0))[:ROWS]
    for part, buf, recv_sem in ((1, k_buf, k_recv), (0, q_buf, q_recv)):
        rate = rates[:, part:part + 1]
        for j in range(HEADS_DEV):
            cols = slice(j * DH, (j + 1) * DH)
            stage[part, j] = (raw[part, :, cols] * rate * gain_ref[part:part + 1, cols]).astype(jnp.bfloat16)
        send_part(part, buf, recv_sem)

    active = jnp.logical_and(z - y >= 0, z - y <= 2)
    slot = jnp.where(active, z - y, 0)

    @pl.when(active)
    def _():
        forwards = []
        for kind, (buf, recv_sem) in enumerate(((v_buf, v_recv), (k_buf, k_recv))):
            for s in range(ZS):
                arrived(buf.at[0, s], recv_sem.at[s])
                copy = remote(
                    buf.at[0, s], buf.at[1, s], f_send.at[kind, s], recv_sem.at[ZS + s], queue, sib
                )
                copy.start()
                forwards.append(copy)
        for s in range(ZS):
            arrived(q_buf.at[s], q_recv.at[s])
        for buf, recv_sem in ((v_buf, v_recv), (k_buf, k_recv)):
            for s in range(ZS):
                arrived(buf.at[1, s], recv_sem.at[ZS + s])
        keys = k_buf[...].reshape(2 * ZS * ROWS, DH)
        vals = v_buf[...].reshape(2 * ZS * ROWS, DH)
        column = lax.broadcasted_iota(jnp.int32, (1, 2 * ZS * ROWS), 1)
        frame = jnp.zeros_like(column)
        for t in range(1, 2 * ZS):
            frame += jnp.where(column >= t * ROWS, 1 if t != ZS else 1 - ZS, 0)
        key_pos = frame - offset
        key_pos = jnp.where(key_pos < 0, key_pos + ZS, key_pos)
        outs = []
        for s in range(ZS):
            bias = jnp.where(key_pos <= position_of(s), 0.0, -1e30)
            scores = lax.dot_general(
                q_buf[s], keys, (((1,), (1,)), ((), ())), preferred_element_type=jnp.float32
            )
            scores = scores * DH ** (-0.5) + bias
            top = jnp.max(scores, axis=1, keepdims=True)
            e = jnp.exp(scores - top)
            total = jnp.sum(e, axis=1, keepdims=True)
            added = jnp.dot(e.astype(jnp.bfloat16), vals, preferred_element_type=jnp.float32)
            o_buf[s] = (added / total).astype(jnp.bfloat16)
            mine = is_self(s)
            far = remote(
                o_buf.at[s], a_buf.at[slot], o_send.at[s], o_recv.at[slot], s * 2 + c, swap_head
            )
            near = pltpu.make_async_copy(o_buf.at[s], a_buf.at[slot], o_recv.at[slot])
            pl.when(mine)(near.start)
            pl.when(jnp.logical_not(mine))(far.start)
            outs.append((mine, far))
        for copy in forwards:
            copy.wait_send()
        for mine, far in outs:
            pl.when(jnp.logical_not(mine))(far.wait_send)

    loads[2].wait()
    for j in range(HEADS_DEV):
        arrived(a_buf.at[j], o_recv.at[j])
    attn = jnp.concatenate([a_buf[j] for j in range(HEADS_DEV)], axis=1)

    def out_block(r):
        return jnp.dot(attn, wo_v[:, columns(r)], preferred_element_type=jnp.float32)

    p_send[0] = out_block(3).astype(jnp.bfloat16)
    send_a = remote(p_send.at[0], rs_buf.at[0], rs_send.at[0], rs_recv.at[0], queue, sib)
    send_a.start()
    ahead = out_block(2)
    p_send[1] = out_block(1).astype(jnp.bfloat16)
    send_b = remote(p_send.at[1], rs_buf.at[1], rs_send.at[1], rs_recv.at[1], queue, sib)
    send_b.start()
    arrived(rs_buf.at[0], rs_recv.at[0])
    p_send[2] = (ahead + rs_buf[0].astype(jnp.float32)).astype(jnp.bfloat16)
    send_c = remote(p_send.at[2], rs_buf.at[2], rs_send.at[2], rs_recv.at[2], queue, xnb)
    send_c.start()
    proj = out_block(0)
    arrived(rs_buf.at[1], rs_recv.at[1])
    proj += rs_buf[1].astype(jnp.float32)
    gate = mod_v[2, pl.ds(level, 1), columns(0)]
    arrived(rs_buf.at[2], rs_recv.at[2])
    proj += rs_buf[2].astype(jnp.float32)
    upd[...] = (lat_ref[...].astype(jnp.float32) + gate * proj).astype(jnp.bfloat16)
    move = remote(upd, fin, mv_send, mv_recv, below, head)
    move.start()
    for copy in (to_x, to_sib, forward, *stats, send_a, send_b, send_c):
        copy.wait_send()
    for mine, far in sends:
        pl.when(jnp.logical_not(mine))(far.wait_send)
    move.wait_send()
    arrived(fin, mv_recv)
    out_ref[...] = fin[...]


def local_fused(latents, fresh_frame, noise_level, offset, mod_table, w_qkv, w_out, q_gain, k_gain):
    bf16, f32 = jnp.bfloat16, jnp.float32
    dma = pltpu.SemaphoreType.DMA
    smem = pl.BlockSpec(memory_space=pltpu.SMEM)
    vmem = pl.BlockSpec(memory_space=pltpu.VMEM)
    hbm = pl.BlockSpec(memory_space=pl.ANY)
    moved = pl.pallas_call(
        block_kernel,
        out_shape=jax.ShapeDtypeStruct((ROWS, WIDTH), bf16),
        in_specs=[smem, smem, vmem, vmem, hbm, hbm, hbm],
        out_specs=vmem,
        scratch_shapes=[
            pltpu.VMEM((3, D, WIDTH), bf16),
            pltpu.VMEM((WIDTH, D), bf16),
            pltpu.VMEM((3, mod_table.shape[0], D), f32),
            pltpu.VMEM((4, ROWS, WIDTH), bf16),
            pltpu.VMEM((ROWS, D), bf16),
            pltpu.VMEM((2, ROWS, WIDTH), f32),
            pltpu.VMEM((4, 8, 256), f32),
            pltpu.VMEM((3, HEADS_DEV, ROWS, DH), bf16),
            pltpu.VMEM((ZS, ROWS, DH), bf16),
            pltpu.VMEM((2, ZS, ROWS, DH), bf16),
            pltpu.VMEM((2, ZS, ROWS, DH), bf16),
            pltpu.VMEM((ZS, ROWS, DH), bf16),
            pltpu.VMEM((HEADS_DEV, ROWS, DH), bf16),
            pltpu.VMEM((3, ROWS, WIDTH), bf16),
            pltpu.VMEM((3, ROWS, WIDTH), bf16),
            pltpu.VMEM((ROWS, WIDTH), bf16),
            pltpu.VMEM((ROWS, WIDTH), bf16),
            dma((3,)),
            dma((3,)),
            dma((4,)),
            dma((4,)),
            dma((4,)),
            dma((3, HEADS_DEV)),
            dma((ZS,)),
            dma((2 * ZS,)),
            dma((2 * ZS,)),
            dma((2, ZS)),
            dma((ZS,)),
            dma((HEADS_DEV,)),
            dma((3,)),
            dma((3,)),
            dma,
            dma,
        ],
        compiler_params=pltpu.CompilerParams(
            collective_id=0, has_side_effects=True, vmem_limit_bytes=48 * 1024 * 1024
        ),
    )(
        noise_level,
        offset,
        latents,
        jnp.stack((q_gain, k_gain)),
        jnp.transpose(w_qkv, (1, 0, 2)),
        w_out,
        jnp.transpose(mod_table, (1, 0, 2)),
    )
    my_slab = lax.axis_index("queue")
    entry_slot = jnp.mod(offset[0] - 1, ZS)
    fresh_half = lax.dynamic_slice_in_dim(fresh_frame, my_slab % 2 * ROWS, ROWS, 0)
    return jnp.where(my_slab // 2 == entry_slot, fresh_half, moved)


def solution(mesh):
    fits = mesh.shape["queue"] == 2 * ZS and mesh.shape["head"] == 4
    return jax.shard_map(
        local_fused if fits else local,
        mesh=mesh,
        in_specs=(
            P("queue", "head"),
            P(None, "head"),
            P(),
            P(),
            P(),
            P(None, None, "head"),
            P("head", None),
            P("head"),
            P("head"),
        ),
        out_specs=P("queue", "head"),
        check_vma=False,
    )
```

```python
import math
import jax
import jax.numpy as jnp
from jax import lax
from jax.experimental import pallas as pl
from jax.experimental.pallas import tpu as pltpu
from jax.sharding import PartitionSpec as P

D = 1536
DH = 128


def passed_along(block, axis, distance):
    devices = range(lax.axis_size(axis))
    route = [((i - distance) % len(devices), i) for i in devices]
    return lax.ppermute(block, axis, route)


def attend(carried, queries, key_block, value_block, allowed):
    run_max, run_total, running = carried
    key_count = key_block.shape[0]
    head_count = queries.shape[1]
    key_heads = key_block.reshape(key_count, head_count, DH)
    value_heads = value_block.reshape(key_count, head_count, DH)
    scores = jnp.einsum(
        "qhd,khd->hqk", queries, key_heads, preferred_element_type=jnp.float32
    ) * DH ** (-0.5)
    scores = jnp.where(allowed[None, None, :], scores, -jnp.inf)
    new_max = jnp.maximum(run_max, jnp.max(scores, axis=2))
    rescale = jnp.exp(run_max - new_max)
    exp_scores = jnp.exp(scores - new_max[:, :, None])
    new_total = run_total * rescale + jnp.sum(exp_scores, axis=2)
    added = jnp.einsum(
        "hqk,khd->hqd",
        exp_scores.astype(jnp.bfloat16),
        value_heads,
        preferred_element_type=jnp.float32,
    )
    return (new_max, new_total, running * rescale[:, :, None] + added)


def local(latents, fresh_frame, noise_level, offset, mod_table, w_qkv, w_out, q_gain, k_gain):
    slabs = lax.axis_size("queue")
    frames = slabs // 2
    my_slab = lax.axis_index("queue")
    my_frame = my_slab // 2
    position = jnp.mod(my_frame - offset[0], frames)
    my_level = noise_level[position]
    modulation = lax.dynamic_index_in_dim(mod_table, my_level, 0, keepdims=False)
    whole = lax.all_gather(latents, "head", axis=1, tiled=True).astype(jnp.float32)
    row_count = whole.shape[0]
    centered = whole - jnp.mean(whole, axis=1, keepdims=True)
    variance = jnp.mean(centered * centered, axis=1, keepdims=True)
    normed = centered * lax.rsqrt(variance + 1e-06)
    modded = (normed * (1.0 + modulation[1]) + modulation[0]).astype(jnp.bfloat16)
    local_width = w_qkv.shape[2]
    projected = jnp.dot(
        modded, w_qkv.reshape(w_qkv.shape[0], 3 * local_width), preferred_element_type=jnp.float32
    )
    projected = projected.reshape(row_count, 3, local_width)
    query_raw = projected[:, 0]
    key_raw = projected[:, 1]
    values = projected[:, 2].astype(jnp.bfloat16)
    query_sq, key_sq = lax.psum(
        (jnp.sum(query_raw * query_raw, axis=1), jnp.sum(key_raw * key_raw, axis=1)), "head"
    )
    queries = (query_raw * lax.rsqrt(query_sq / D + 1e-06)[:, None] * q_gain).astype(jnp.bfloat16)
    key_normed = (key_raw * lax.rsqrt(key_sq / D + 1e-06)[:, None] * k_gain).astype(jnp.bfloat16)
    head_count = local_width // DH
    query_heads = queries.reshape(row_count, head_count, DH)
    start_state = (
        jnp.full((head_count, row_count), -1e30, jnp.float32),
        jnp.zeros((head_count, row_count), jnp.float32),
        jnp.zeros((head_count, row_count, DH), jnp.float32),
    )
    all_rows = jnp.ones((row_count,), dtype=bool)
    carried = attend(start_state, query_heads, key_normed, values, all_rows)
    stacked = jnp.stack((key_normed, values))

    def pass_step(turn, loop_state):
        pieces, state_now = loop_state
        pieces = passed_along(pieces, "queue", 1)
        key_slab = jnp.mod(my_slab - turn, slabs)
        key_pos = jnp.mod(key_slab // 2 - offset[0], frames)

        def use_piece(state_in):
            return attend(state_in, query_heads, pieces[0], pieces[1], all_rows)

        def keep_state(state_in):
            return state_in

        state_now = lax.cond(key_pos <= position, use_piece, keep_state, state_now)
        return (pieces, state_now)

    stacked, carried = lax.fori_loop(1, slabs, pass_step, (stacked, carried))
    run_max, run_total, running = carried
    attn = (
        jnp.transpose(running / run_total[:, :, None], (1, 0, 2))
        .reshape(row_count, local_width)
        .astype(jnp.bfloat16)
    )
    partial_out = jnp.dot(attn, w_out, preferred_element_type=jnp.float32)
    proj = lax.psum_scatter(
        partial_out.astype(jnp.bfloat16), "head", scatter_dimension=1, tiled=True
    ).astype(jnp.float32)
    feature_start = lax.axis_index("head") * local_width
    gate_local = lax.dynamic_slice_in_dim(modulation[2], feature_start, local_width)
    updated = (latents.astype(jnp.float32) + gate_local * proj).astype(jnp.bfloat16)
    moved = passed_along(updated, "queue", -2)
    entry_slot = jnp.mod(offset[0] - 1, frames)
    fresh_half = lax.dynamic_slice_in_dim(fresh_frame, my_slab % 2 * row_count, row_count, 0)
    return jnp.where(my_frame == entry_slot, fresh_half, moved)


MESH = pl.DeviceIdType.MESH
ZS = 4
ROWS = 192
WIDTH = 384
HEADS_DEV = 3
PIECES = 2
VMEM_BYTES = 64 * 1024 * 1024 - 128 * 1024
PIECE = ROWS // PIECES


def arrived(buffer, sem):
    pltpu.make_async_copy(buffer, buffer, sem).wait()


def block_kernel(
    offset_ref, noise_hbm, lat_hbm, q_gain_hbm, k_gain_hbm, w_hbm, wout_hbm, mod_hbm, out_ref,
    noise_ref, lat_ref, q_gain, k_gain,
    w_v, wo_v, mod_v, lat_buf, mod_act, raw, stat_buf, stage, q_buf, k_buf, v_buf,
    o_buf, a_buf, p_send, rs_buf, upd, fin,
    load_sem, lat_send, lat_recv, st_send, st_recv, qkv_send, q_recv, k_recv, v_recv,
    f_send, o_send, o_recv, rs_send, rs_recv, mv_send, mv_recv,
):
    queue = lax.axis_index("queue")
    head = lax.axis_index("head")
    z, y = queue // 2, queue % 2
    x, c = head // 2, head % 2
    sib = x * 2 + (1 - c)
    xnb = (1 - x) * 2 + c
    diag = (1 - x) * 2 + (1 - c)
    peers = (head, sib, xnb, diag)
    below = queue - 2 + jnp.where(z == 0, 2 * ZS, 0)
    above = queue + 2 - jnp.where(z == ZS - 1, 2 * ZS, 0)
    swap_head = x * 2 + y
    on_diagonal = y == c

    def is_self(zt):
        return jnp.logical_and(on_diagonal, zt == z)

    loads = [
        pltpu.make_async_copy(mod_hbm, mod_v, load_sem.at[0]),
        pltpu.make_async_copy(w_hbm, w_v, load_sem.at[1]),
        pltpu.make_async_copy(wout_hbm, wo_v, load_sem.at[2]),
        pltpu.make_async_copy(lat_hbm, lat_ref, load_sem.at[3]),
        pltpu.make_async_copy(noise_hbm, noise_ref, load_sem.at[4]),
        pltpu.make_async_copy(q_gain_hbm, q_gain, load_sem.at[5]),
        pltpu.make_async_copy(k_gain_hbm, k_gain, load_sem.at[6]),
    ]
    for load in loads:
        load.start()

    barrier = pltpu.get_barrier_semaphore()

    def greet(q_id, h_id):
        pl.semaphore_signal(barrier, inc=1, device_id=(q_id, h_id), device_id_type=MESH)

    for peer in peers[1:]:
        greet(queue, peer)
    greet(below, head)
    greet(above, head)
    for zt in range(ZS):
        pl.when(jnp.logical_not(is_self(zt)))(lambda zt=zt: greet(zt * 2 + c, swap_head))
    pl.semaphore_wait(barrier, 5 + ZS - jnp.where(on_diagonal, 1, 0))

    def remote(src, dst, s_sem, r_sem, q_id, h_id):
        return pltpu.make_async_remote_copy(
            src_ref=src, dst_ref=dst, send_sem=s_sem, recv_sem=r_sem,
            device_id=(q_id, h_id), device_id_type=MESH,
        )

    loads[3].wait()
    pieces = [pl.ds(p * PIECE, PIECE) for p in range(PIECES)]
    to_x, forward = [], []
    for p, rows in enumerate(pieces):
        to_x.append(remote(
            lat_ref.at[rows], lat_buf.at[2, rows], lat_send.at[0, p], lat_recv.at[2, p], queue, xnb
        ))
        to_x[p].start()
        forward.append(remote(
            lat_buf.at[2, rows], lat_buf.at[3, rows], lat_send.at[2, p], lat_recv.at[3, p], queue, sib
        ))
    to_sib = remote(lat_ref, lat_buf.at[1], lat_send.at[1, 0], lat_recv.at[1, 0], queue, sib)
    to_sib.start()
    for p, rows in enumerate(pieces):
        arrived(lat_buf.at[2, rows], lat_recv.at[2, p])
        forward[p].start()
    arrived(lat_buf.at[1], lat_recv.at[1, 0])
    loads[0].wait()
    for load in loads[4:]:
        load.wait()

    offset = lax.rem(offset_ref[0], ZS)

    def position_of(frame):
        return lax.rem(frame + ZS - offset, ZS)

    level = noise_ref[position_of(z)]
    for p, rows in enumerate(pieces):
        arrived(lat_buf.at[3, rows], lat_recv.at[3, p])

    def block(r):
        return (lat_ref[...] if r == 0 else lat_buf[r]).astype(jnp.float32)

    def columns(r):
        return pl.ds(pl.multiple_of(peers[r] * WIDTH, WIDTH), WIDTH)

    mean = sum(jnp.sum(block(r), axis=1, keepdims=True) for r in range(4)) / D
    square = jnp.zeros((ROWS, 1), jnp.float32)
    for r in range(4):
        centered = block(r) - mean
        square += jnp.sum(centered * centered, axis=1, keepdims=True)
    inv = lax.rsqrt(square / D + 1e-06)
    for r in range(4):
        shift = mod_v[0, pl.ds(level, 1), columns(r)]
        scale = mod_v[1, pl.ds(level, 1), columns(r)]
        normed = (block(r) - mean) * inv
        mod_act[:, columns(r)] = (normed * (1.0 + scale) + shift).astype(jnp.bfloat16)

    loads[1].wait()
    sends = []

    def send_part(part, buf, recv_sem):
        for j in range(HEADS_DEV):
            zt = j + c
            mine = is_self(zt)
            src = stage.at[part, j]
            dst = buf.at[z] if part == 0 else buf.at[0, z]
            far = remote(src, dst, qkv_send.at[part, j], recv_sem.at[z], zt * 2 + c, swap_head)
            near = pltpu.make_async_copy(src, dst, recv_sem.at[z])
            pl.when(mine)(near.start)
            pl.when(jnp.logical_not(mine))(far.start)
            sends.append((mine, far))

    values = jnp.dot(mod_act[...], w_v[2], preferred_element_type=jnp.float32)
    for j in range(HEADS_DEV):
        stage[2, j] = values[:, j * DH:(j + 1) * DH].astype(jnp.bfloat16)
    send_part(2, v_buf, v_recv)

    sums = []
    for i in range(2):
        projected = jnp.dot(mod_act[...], w_v[i], preferred_element_type=jnp.float32)
        raw[i] = projected
        sums.append(jnp.sum(projected * projected, axis=1, keepdims=True))
    lane = lax.broadcasted_iota(jnp.int32, (256, 128), 1)
    padding = jnp.zeros((256 - ROWS, 1), jnp.float32)
    spread = jnp.where(
        lane == 0,
        jnp.concatenate([sums[0], padding], axis=0),
        jnp.concatenate([sums[1], padding], axis=0),
    )
    stat_buf[0] = jnp.transpose(spread)[:8]
    stats = [
        remote(stat_buf.at[0], stat_buf.at[r], st_send.at[r], st_recv.at[r], queue, peers[r])
        for r in (2, 3, 1)
    ]
    for copy in stats:
        copy.start()

    for r in (1, 2, 3):
        arrived(stat_buf.at[r], st_recv.at[r])
    total_sq = stat_buf[0] + stat_buf[1] + stat_buf[2] + stat_buf[3]
    rates = lax.rsqrt(total_sq / D + 1e-06)
    rates = jnp.transpose(jnp.concatenate([rates] * 16, axis=0))[:ROWS]
    for part, buf, recv_sem in ((1, k_buf, k_recv), (0, q_buf, q_recv)):
        rate = rates[:, part:part + 1]
        gain = (q_gain, k_gain)[part][...].reshape(1, WIDTH)
        for j in range(HEADS_DEV):
            cols = slice(j * DH, (j + 1) * DH)
            stage[part, j] = (raw[part, :, cols] * rate * gain[:, cols]).astype(jnp.bfloat16)
        send_part(part, buf, recv_sem)

    active = jnp.logical_and(z - y >= 0, z - y <= 2)
    slot = jnp.where(active, z - y, 0)

    @pl.when(active)
    def _():
        forwards = []
        for kind, (buf, recv_sem) in enumerate(((v_buf, v_recv), (k_buf, k_recv))):
            for s in range(ZS):
                arrived(buf.at[0, s], recv_sem.at[s])
                copy = remote(
                    buf.at[0, s], buf.at[1, s], f_send.at[kind, s], recv_sem.at[ZS + s], queue, sib
                )
                copy.start()
                forwards.append(copy)
        for s in range(ZS):
            arrived(q_buf.at[s], q_recv.at[s])
        for buf, recv_sem in ((v_buf, v_recv), (k_buf, k_recv)):
            for s in range(ZS):
                arrived(buf.at[1, s], recv_sem.at[ZS + s])
        keys = k_buf[...].reshape(2 * ZS * ROWS, DH)
        vals = v_buf[...].reshape(2 * ZS * ROWS, DH)
        column = lax.broadcasted_iota(jnp.int32, (1, 2 * ZS * ROWS), 1)
        frame = jnp.zeros_like(column)
        for t in range(1, 2 * ZS):
            frame += jnp.where(column >= t * ROWS, 1 if t != ZS else 1 - ZS, 0)
        key_pos = frame - offset
        key_pos = jnp.where(key_pos < 0, key_pos + ZS, key_pos)
        outs = []
        for s in range(ZS):
            bias = jnp.where(key_pos <= position_of(s), 0.0, -1e30)
            scores = lax.dot_general(
                q_buf[s], keys, (((1,), (1,)), ((), ())), preferred_element_type=jnp.float32
            )
            scores = scores * (DH ** (-0.5) * math.log2(math.e)) + bias
            top = jnp.max(scores, axis=1, keepdims=True)
            e = jnp.exp2(scores - top)
            total = jnp.sum(e, axis=1, keepdims=True)
            added = jnp.dot(e.astype(jnp.bfloat16), vals, preferred_element_type=jnp.float32)
            o_buf[s] = (added / total).astype(jnp.bfloat16)
            mine = is_self(s)
            far = remote(
                o_buf.at[s], a_buf.at[slot], o_send.at[s], o_recv.at[slot], s * 2 + c, swap_head
            )
            near = pltpu.make_async_copy(o_buf.at[s], a_buf.at[slot], o_recv.at[slot])
            pl.when(mine)(near.start)
            pl.when(jnp.logical_not(mine))(far.start)
            outs.append((mine, far))
        for copy in forwards:
            copy.wait_send()
        for mine, far in outs:
            pl.when(jnp.logical_not(mine))(far.wait_send)

    loads[2].wait()
    for j in range(HEADS_DEV):
        arrived(a_buf.at[j], o_recv.at[j])
    attn = jnp.concatenate([a_buf[j] for j in range(HEADS_DEV)], axis=1)

    def out_block(r):
        return jnp.dot(attn, wo_v[:, columns(r)], preferred_element_type=jnp.float32)

    def rs_copy(kind, p, q_id, h_id):
        rows = pieces[p]
        return remote(
            p_send.at[kind, rows], rs_buf.at[kind, rows], rs_send.at[kind, p], rs_recv.at[kind, p], q_id, h_id
        )

    send_a, send_b, send_c, moves = [], [], [], []
    p_send[0] = out_block(3).astype(jnp.bfloat16)
    for p in range(PIECES):
        send_a.append(rs_copy(0, p, queue, sib))
        send_a[p].start()
    ahead = out_block(2)
    p_send[1] = out_block(1).astype(jnp.bfloat16)
    for p in range(PIECES):
        send_b.append(rs_copy(1, p, queue, sib))
        send_b[p].start()
    for p, rows in enumerate(pieces):
        arrived(rs_buf.at[0, rows], rs_recv.at[0, p])
        mine = ahead[p * PIECE:(p + 1) * PIECE]
        p_send[2, rows] = (mine + rs_buf[0, rows].astype(jnp.float32)).astype(jnp.bfloat16)
        send_c.append(rs_copy(2, p, queue, xnb))
        send_c[p].start()
    proj = out_block(0)
    gate = mod_v[2, pl.ds(level, 1), columns(0)]
    for p, rows in enumerate(pieces):
        arrived(rs_buf.at[1, rows], rs_recv.at[1, p])
    proj += rs_buf[1].astype(jnp.float32)
    for p, rows in enumerate(pieces):
        arrived(rs_buf.at[2, rows], rs_recv.at[2, p])
        full = proj[p * PIECE:(p + 1) * PIECE] + rs_buf[2, rows].astype(jnp.float32)
        upd[rows] = (lat_ref[rows].astype(jnp.float32) + gate * full).astype(jnp.bfloat16)
        moves.append(remote(upd.at[rows], fin.at[rows], mv_send.at[p], mv_recv.at[p], below, head))
        moves[p].start()
    for copy in (*to_x, to_sib, *forward, *stats, *send_a, *send_b, *send_c, *moves):
        copy.wait_send()
    for mine, far in sends:
        pl.when(jnp.logical_not(mine))(far.wait_send)
    for p, rows in enumerate(pieces):
        arrived(fin.at[rows], mv_recv.at[p])
        out_ref[rows] = fin[rows]


def local_fused(latents, fresh_frame, noise_level, offset, mod_table, w_qkv, w_out, q_gain, k_gain):
    bf16, f32 = jnp.bfloat16, jnp.float32
    dma = pltpu.SemaphoreType.DMA
    vmem = pl.BlockSpec(memory_space=pltpu.VMEM)
    hbm = pl.BlockSpec(memory_space=pl.ANY)
    moved = pl.pallas_call(
        block_kernel,
        out_shape=jax.ShapeDtypeStruct((ROWS, WIDTH), bf16),
        in_specs=[pl.BlockSpec(memory_space=pltpu.SMEM)] + [hbm] * 7,
        out_specs=vmem,
        scratch_shapes=[
            pltpu.SMEM(noise_level.shape, jnp.int32),
            pltpu.VMEM((ROWS, WIDTH), bf16),
            pltpu.VMEM((WIDTH,), f32),
            pltpu.VMEM((WIDTH,), f32),
            pltpu.VMEM((3, D, WIDTH), bf16),
            pltpu.VMEM((WIDTH, D), bf16),
            pltpu.VMEM((3, mod_table.shape[0], D), f32),
            pltpu.VMEM((4, ROWS, WIDTH), bf16),
            pltpu.VMEM((ROWS, D), bf16),
            pltpu.VMEM((2, ROWS, WIDTH), f32),
            pltpu.VMEM((4, 8, 256), f32),
            pltpu.VMEM((3, HEADS_DEV, ROWS, DH), bf16),
            pltpu.VMEM((ZS, ROWS, DH), bf16),
            pltpu.VMEM((2, ZS, ROWS, DH), bf16),
            pltpu.VMEM((2, ZS, ROWS, DH), bf16),
            pltpu.VMEM((ZS, ROWS, DH), bf16),
            pltpu.VMEM((HEADS_DEV, ROWS, DH), bf16),
            pltpu.VMEM((3, ROWS, WIDTH), bf16),
            pltpu.VMEM((3, ROWS, WIDTH), bf16),
            pltpu.VMEM((ROWS, WIDTH), bf16),
            pltpu.VMEM((ROWS, WIDTH), bf16),
            dma((7,)),
            dma((3, PIECES)),
            dma((4, PIECES)),
            dma((4,)),
            dma((4,)),
            dma((3, HEADS_DEV)),
            dma((ZS,)),
            dma((2 * ZS,)),
            dma((2 * ZS,)),
            dma((2, ZS)),
            dma((ZS,)),
            dma((HEADS_DEV,)),
            dma((3, PIECES)),
            dma((3, PIECES)),
            dma((PIECES,)),
            dma((PIECES,)),
        ],
        compiler_params=pltpu.CompilerParams(
            collective_id=0, has_side_effects=True, vmem_limit_bytes=VMEM_BYTES
        ),
    )(
        offset,
        noise_level,
        latents,
        q_gain,
        k_gain,
        jnp.transpose(w_qkv, (1, 0, 2)),
        w_out,
        jnp.transpose(mod_table, (1, 0, 2)),
    )
    my_slab = lax.axis_index("queue")
    entry_slot = jnp.mod(offset[0] - 1, ZS)
    fresh_half = lax.dynamic_slice_in_dim(fresh_frame, my_slab % 2 * ROWS, ROWS, 0)
    return jnp.where(my_slab // 2 == entry_slot, fresh_half, moved)


def solution(mesh):
    fits = mesh.shape["queue"] == 2 * ZS and mesh.shape["head"] == 4
    return jax.shard_map(
        local_fused if fits else local,
        mesh=mesh,
        in_specs=(
            P("queue", "head"),
            P(None, "head"),
            P(),
            P(),
            P(),
            P(None, None, "head"),
            P("head", None),
            P("head"),
            P("head"),
        ),
        out_specs=P("queue", "head"),
        check_vma=False,
    )
```

```python
import math
import jax
import jax.numpy as jnp
from jax import lax
from jax.experimental import pallas as pl
from jax.experimental.pallas import tpu as pltpu
from jax.sharding import PartitionSpec as P

D = 1536
DH = 128


def passed_along(block, axis, distance):
    devices = range(lax.axis_size(axis))
    route = [((i - distance) % len(devices), i) for i in devices]
    return lax.ppermute(block, axis, route)


def attend(carried, queries, key_block, value_block, allowed):
    run_max, run_total, running = carried
    key_count = key_block.shape[0]
    head_count = queries.shape[1]
    key_heads = key_block.reshape(key_count, head_count, DH)
    value_heads = value_block.reshape(key_count, head_count, DH)
    scores = jnp.einsum(
        "qhd,khd->hqk", queries, key_heads, preferred_element_type=jnp.float32
    ) * DH ** (-0.5)
    scores = jnp.where(allowed[None, None, :], scores, -jnp.inf)
    new_max = jnp.maximum(run_max, jnp.max(scores, axis=2))
    rescale = jnp.exp(run_max - new_max)
    exp_scores = jnp.exp(scores - new_max[:, :, None])
    new_total = run_total * rescale + jnp.sum(exp_scores, axis=2)
    added = jnp.einsum(
        "hqk,khd->hqd",
        exp_scores.astype(jnp.bfloat16),
        value_heads,
        preferred_element_type=jnp.float32,
    )
    return (new_max, new_total, running * rescale[:, :, None] + added)


def local(latents, fresh_frame, noise_level, offset, mod_table, w_qkv, w_out, q_gain, k_gain):
    slabs = lax.axis_size("queue")
    frames = slabs // 2
    my_slab = lax.axis_index("queue")
    my_frame = my_slab // 2
    position = jnp.mod(my_frame - offset[0], frames)
    my_level = noise_level[position]
    modulation = lax.dynamic_index_in_dim(mod_table, my_level, 0, keepdims=False)
    whole = lax.all_gather(latents, "head", axis=1, tiled=True).astype(jnp.float32)
    row_count = whole.shape[0]
    centered = whole - jnp.mean(whole, axis=1, keepdims=True)
    variance = jnp.mean(centered * centered, axis=1, keepdims=True)
    normed = centered * lax.rsqrt(variance + 1e-06)
    modded = (normed * (1.0 + modulation[1]) + modulation[0]).astype(jnp.bfloat16)
    local_width = w_qkv.shape[2]
    projected = jnp.dot(
        modded, w_qkv.reshape(w_qkv.shape[0], 3 * local_width), preferred_element_type=jnp.float32
    )
    projected = projected.reshape(row_count, 3, local_width)
    query_raw = projected[:, 0]
    key_raw = projected[:, 1]
    values = projected[:, 2].astype(jnp.bfloat16)
    query_sq, key_sq = lax.psum(
        (jnp.sum(query_raw * query_raw, axis=1), jnp.sum(key_raw * key_raw, axis=1)), "head"
    )
    queries = (query_raw * lax.rsqrt(query_sq / D + 1e-06)[:, None] * q_gain).astype(jnp.bfloat16)
    key_normed = (key_raw * lax.rsqrt(key_sq / D + 1e-06)[:, None] * k_gain).astype(jnp.bfloat16)
    head_count = local_width // DH
    query_heads = queries.reshape(row_count, head_count, DH)
    start_state = (
        jnp.full((head_count, row_count), -1e30, jnp.float32),
        jnp.zeros((head_count, row_count), jnp.float32),
        jnp.zeros((head_count, row_count, DH), jnp.float32),
    )
    all_rows = jnp.ones((row_count,), dtype=bool)
    carried = attend(start_state, query_heads, key_normed, values, all_rows)
    stacked = jnp.stack((key_normed, values))

    def pass_step(turn, loop_state):
        pieces, state_now = loop_state
        pieces = passed_along(pieces, "queue", 1)
        key_slab = jnp.mod(my_slab - turn, slabs)
        key_pos = jnp.mod(key_slab // 2 - offset[0], frames)

        def use_piece(state_in):
            return attend(state_in, query_heads, pieces[0], pieces[1], all_rows)

        def keep_state(state_in):
            return state_in

        state_now = lax.cond(key_pos <= position, use_piece, keep_state, state_now)
        return (pieces, state_now)

    stacked, carried = lax.fori_loop(1, slabs, pass_step, (stacked, carried))
    run_max, run_total, running = carried
    attn = (
        jnp.transpose(running / run_total[:, :, None], (1, 0, 2))
        .reshape(row_count, local_width)
        .astype(jnp.bfloat16)
    )
    partial_out = jnp.dot(attn, w_out, preferred_element_type=jnp.float32)
    proj = lax.psum_scatter(
        partial_out.astype(jnp.bfloat16), "head", scatter_dimension=1, tiled=True
    ).astype(jnp.float32)
    feature_start = lax.axis_index("head") * local_width
    gate_local = lax.dynamic_slice_in_dim(modulation[2], feature_start, local_width)
    updated = (latents.astype(jnp.float32) + gate_local * proj).astype(jnp.bfloat16)
    moved = passed_along(updated, "queue", -2)
    entry_slot = jnp.mod(offset[0] - 1, frames)
    fresh_half = lax.dynamic_slice_in_dim(fresh_frame, my_slab % 2 * row_count, row_count, 0)
    return jnp.where(my_frame == entry_slot, fresh_half, moved)


MESH = pl.DeviceIdType.MESH
ZS = 4
ROWS = 192
WIDTH = 384
HEADS_DEV = 3
PIECES = 2
VMEM_BYTES = 64 * 1024 * 1024 - 128 * 1024
PIECE = ROWS // PIECES


def arrived(buffer, sem):
    pltpu.make_async_copy(buffer, buffer, sem).wait()


def block_kernel(
    offset_ref, noise_hbm, lat_hbm, q_gain_hbm, k_gain_hbm, w_hbm, wout_hbm, mod_hbm, out_ref,
    noise_ref, lat_ref, q_gain, k_gain,
    w_v, wo_v, mod_v, lat_buf, mod_act, raw, stat_buf, stage, q_buf, k_buf, v_buf,
    o_buf, a_buf, p_send, rs_buf, s_buf, lat_next,
    load_sem, lat_send, lat_recv, st_send, st_recv, qkv_send, q_recv, k_recv, v_recv,
    f_send, o_send, o_recv, rs_send, rs_recv, mv_send, mv_recv,
):
    queue = lax.axis_index("queue")
    head = lax.axis_index("head")
    z, y = queue // 2, queue % 2
    x, c = head // 2, head % 2
    sib = x * 2 + (1 - c)
    xnb = (1 - x) * 2 + c
    diag = (1 - x) * 2 + (1 - c)
    peers = (head, sib, xnb, diag)
    below = queue - 2 + jnp.where(z == 0, 2 * ZS, 0)
    above = queue + 2 - jnp.where(z == ZS - 1, 2 * ZS, 0)
    swap_head = x * 2 + y
    on_diagonal = y == c

    def is_self(zt):
        return jnp.logical_and(on_diagonal, zt == z)

    loads = [
        pltpu.make_async_copy(mod_hbm, mod_v, load_sem.at[0]),
        pltpu.make_async_copy(w_hbm, w_v, load_sem.at[1]),
        pltpu.make_async_copy(wout_hbm, wo_v, load_sem.at[2]),
        pltpu.make_async_copy(lat_hbm, lat_ref, load_sem.at[3]),
        pltpu.make_async_copy(noise_hbm, noise_ref, load_sem.at[4]),
        pltpu.make_async_copy(q_gain_hbm, q_gain, load_sem.at[5]),
        pltpu.make_async_copy(k_gain_hbm, k_gain, load_sem.at[6]),
    ]
    for load in loads:
        load.start()

    barrier = pltpu.get_barrier_semaphore()

    def greet(q_id, h_id):
        pl.semaphore_signal(barrier, inc=1, device_id=(q_id, h_id), device_id_type=MESH)

    for peer in peers[1:]:
        greet(queue, peer)
    greet(below, head)
    greet(above, head)
    for zt in range(ZS):
        pl.when(jnp.logical_not(is_self(zt)))(lambda zt=zt: greet(zt * 2 + c, swap_head))
    pl.semaphore_wait(barrier, 5 + ZS - jnp.where(on_diagonal, 1, 0))

    def remote(src, dst, s_sem, r_sem, q_id, h_id):
        return pltpu.make_async_remote_copy(
            src_ref=src, dst_ref=dst, send_sem=s_sem, recv_sem=r_sem,
            device_id=(q_id, h_id), device_id_type=MESH,
        )

    loads[3].wait()
    pieces = [pl.ds(p * PIECE, PIECE) for p in range(PIECES)]
    to_x, forward = [], []
    for p, rows in enumerate(pieces):
        to_x.append(remote(
            lat_ref.at[rows], lat_buf.at[2, rows], lat_send.at[0, p], lat_recv.at[2, p], queue, xnb
        ))
        to_x[p].start()
        forward.append(remote(
            lat_buf.at[2, rows], lat_buf.at[3, rows], lat_send.at[2, p], lat_recv.at[3, p], queue, sib
        ))
    to_sib = remote(lat_ref, lat_buf.at[1], lat_send.at[1, 0], lat_recv.at[1, 0], queue, sib)
    to_sib.start()
    lat_move = remote(lat_ref, lat_next, mv_send, mv_recv, below, head)
    lat_move.start()
    for p, rows in enumerate(pieces):
        arrived(lat_buf.at[2, rows], lat_recv.at[2, p])
        forward[p].start()
    arrived(lat_buf.at[1], lat_recv.at[1, 0])
    loads[0].wait()
    for load in loads[4:]:
        load.wait()

    offset = lax.rem(offset_ref[0], ZS)

    def position_of(frame):
        return lax.rem(frame + ZS - offset, ZS)

    level = noise_ref[position_of(z)]
    for p, rows in enumerate(pieces):
        arrived(lat_buf.at[3, rows], lat_recv.at[3, p])

    def block(r):
        return (lat_ref[...] if r == 0 else lat_buf[r]).astype(jnp.float32)

    def columns(r):
        return pl.ds(pl.multiple_of(peers[r] * WIDTH, WIDTH), WIDTH)

    mean = sum(jnp.sum(block(r), axis=1, keepdims=True) for r in range(4)) / D
    square = jnp.zeros((ROWS, 1), jnp.float32)
    for r in range(4):
        centered = block(r) - mean
        square += jnp.sum(centered * centered, axis=1, keepdims=True)
    inv = lax.rsqrt(square / D + 1e-06)
    for r in range(4):
        shift = mod_v[0, pl.ds(level, 1), columns(r)]
        scale = mod_v[1, pl.ds(level, 1), columns(r)]
        normed = (block(r) - mean) * inv
        mod_act[:, columns(r)] = (normed * (1.0 + scale) + shift).astype(jnp.bfloat16)

    loads[1].wait()
    sends = []

    def send_part(part, buf, recv_sem):
        for j in range(HEADS_DEV):
            zt = j + c
            mine = is_self(zt)
            src = stage.at[part, j]
            dst = buf.at[z] if part == 0 else buf.at[0, z]
            far = remote(src, dst, qkv_send.at[part, j], recv_sem.at[z], zt * 2 + c, swap_head)
            near = pltpu.make_async_copy(src, dst, recv_sem.at[z])
            pl.when(mine)(near.start)
            pl.when(jnp.logical_not(mine))(far.start)
            sends.append((mine, far))

    values = jnp.dot(mod_act[...], w_v[2], preferred_element_type=jnp.float32)
    for j in range(HEADS_DEV):
        stage[2, j] = values[:, j * DH:(j + 1) * DH].astype(jnp.bfloat16)
    send_part(2, v_buf, v_recv)

    sums = []
    for i in range(2):
        projected = jnp.dot(mod_act[...], w_v[i], preferred_element_type=jnp.float32)
        raw[i] = projected
        sums.append(jnp.sum(projected * projected, axis=1, keepdims=True))
    lane = lax.broadcasted_iota(jnp.int32, (256, 128), 1)
    padding = jnp.zeros((256 - ROWS, 1), jnp.float32)
    spread = jnp.where(
        lane == 0,
        jnp.concatenate([sums[0], padding], axis=0),
        jnp.concatenate([sums[1], padding], axis=0),
    )
    stat_buf[0] = jnp.transpose(spread)[:8]
    stats = [
        remote(stat_buf.at[0], stat_buf.at[r], st_send.at[r], st_recv.at[r], queue, peers[r])
        for r in (2, 3, 1)
    ]
    for copy in stats:
        copy.start()

    for r in (1, 2, 3):
        arrived(stat_buf.at[r], st_recv.at[r])
    total_sq = stat_buf[0] + stat_buf[1] + stat_buf[2] + stat_buf[3]
    rates = lax.rsqrt(total_sq / D + 1e-06)
    rates = jnp.transpose(jnp.concatenate([rates] * 16, axis=0))[:ROWS]
    for part, buf, recv_sem in ((1, k_buf, k_recv), (0, q_buf, q_recv)):
        rate = rates[:, part:part + 1]
        gain = (q_gain, k_gain)[part][...].reshape(1, WIDTH)
        for j in range(HEADS_DEV):
            cols = slice(j * DH, (j + 1) * DH)
            stage[part, j] = (raw[part, :, cols] * rate * gain[:, cols]).astype(jnp.bfloat16)
        send_part(part, buf, recv_sem)

    active = jnp.logical_and(z - y >= 0, z - y <= 2)
    slot = jnp.where(active, z - y, 0)

    @pl.when(active)
    def _():
        forwards = []
        for kind, (buf, recv_sem) in enumerate(((v_buf, v_recv), (k_buf, k_recv))):
            for s in range(ZS):
                arrived(buf.at[0, s], recv_sem.at[s])
                copy = remote(
                    buf.at[0, s], buf.at[1, s], f_send.at[kind, s], recv_sem.at[ZS + s], queue, sib
                )
                copy.start()
                forwards.append(copy)
        for buf, recv_sem in ((v_buf, v_recv), (k_buf, k_recv)):
            for s in range(ZS):
                arrived(buf.at[1, s], recv_sem.at[ZS + s])
        keys = k_buf[...].reshape(2 * ZS * ROWS, DH)
        vals = v_buf[...].reshape(2 * ZS * ROWS, DH)
        column = lax.broadcasted_iota(jnp.int32, (1, 2 * ZS * ROWS), 1)
        frame = jnp.zeros_like(column)
        for t in range(1, 2 * ZS):
            frame += jnp.where(column >= t * ROWS, 1 if t != ZS else 1 - ZS, 0)
        key_pos = frame - offset
        key_pos = jnp.where(key_pos < 0, key_pos + ZS, key_pos)
        order = (z, z + 1 - 2 * (z % 2), (z + 2) % ZS, ZS - 1 - z)

        def score_into(i):
            arrived(q_buf.at[order[i]], q_recv.at[order[i]])
            s_buf[i % 2] = lax.dot_general(
                q_buf[order[i]], keys, (((1,), (1,)), ((), ())), preferred_element_type=jnp.float32
            )

        outs = []
        score_into(0)
        for i, s in enumerate(order):
            if i + 1 < ZS:
                score_into(i + 1)
            bias = jnp.where(key_pos <= position_of(s), 0.0, -1e30)
            scores = s_buf[i % 2] * (DH ** (-0.5) * math.log2(math.e)) + bias
            top = jnp.max(scores, axis=1, keepdims=True)
            e = jnp.exp2(scores - top)
            total = jnp.sum(e, axis=1, keepdims=True)
            added = jnp.dot(e.astype(jnp.bfloat16), vals, preferred_element_type=jnp.float32)
            o_buf[i] = (added / total).astype(jnp.bfloat16)
            zt = (s + ZS - 1) % ZS
            mine = is_self(zt)
            far = remote(
                o_buf.at[i], a_buf.at[slot], o_send.at[i], o_recv.at[slot], zt * 2 + c, swap_head
            )
            near = pltpu.make_async_copy(o_buf.at[i], a_buf.at[slot], o_recv.at[slot])
            pl.when(mine)(near.start)
            pl.when(jnp.logical_not(mine))(far.start)
            outs.append((mine, far))
        for copy in forwards:
            copy.wait_send()
        for mine, far in outs:
            pl.when(jnp.logical_not(mine))(far.wait_send)

    loads[2].wait()
    for j in range(HEADS_DEV):
        arrived(a_buf.at[j], o_recv.at[j])
    attn = jnp.concatenate([a_buf[j] for j in range(HEADS_DEV)], axis=1)

    def out_block(r):
        return jnp.dot(attn, wo_v[:, columns(r)], preferred_element_type=jnp.float32)

    def rs_copy(kind, p, q_id, h_id):
        rows = pieces[p]
        return remote(
            p_send.at[kind, rows], rs_buf.at[kind, rows], rs_send.at[kind, p], rs_recv.at[kind, p], q_id, h_id
        )

    send_a, send_b, send_c = [], [], []
    p_send[0] = out_block(3).astype(jnp.bfloat16)
    for p in range(PIECES):
        send_a.append(rs_copy(0, p, queue, sib))
        send_a[p].start()
    ahead = out_block(2)
    p_send[1] = out_block(1).astype(jnp.bfloat16)
    for p in range(PIECES):
        send_b.append(rs_copy(1, p, queue, sib))
        send_b[p].start()
    for p, rows in enumerate(pieces):
        arrived(rs_buf.at[0, rows], rs_recv.at[0, p])
        mine = ahead[p * PIECE:(p + 1) * PIECE]
        p_send[2, rows] = (mine + rs_buf[0, rows].astype(jnp.float32)).astype(jnp.bfloat16)
        send_c.append(rs_copy(2, p, queue, xnb))
        send_c[p].start()
    proj = out_block(0)
    gate = mod_v[2, pl.ds(noise_ref[position_of((z + 1) % ZS)], 1), columns(0)]
    arrived(lat_next, mv_recv)
    for p, rows in enumerate(pieces):
        arrived(rs_buf.at[1, rows], rs_recv.at[1, p])
    proj += rs_buf[1].astype(jnp.float32)
    for p, rows in enumerate(pieces):
        arrived(rs_buf.at[2, rows], rs_recv.at[2, p])
        full = proj[p * PIECE:(p + 1) * PIECE] + rs_buf[2, rows].astype(jnp.float32)
        out_ref[rows] = (lat_next[rows].astype(jnp.float32) + gate * full).astype(jnp.bfloat16)
    for copy in (*to_x, to_sib, *forward, *stats, *send_a, *send_b, *send_c, lat_move):
        copy.wait_send()
    for mine, far in sends:
        pl.when(jnp.logical_not(mine))(far.wait_send)


def local_fused(latents, fresh_frame, noise_level, offset, mod_table, w_qkv, w_out, q_gain, k_gain):
    bf16, f32 = jnp.bfloat16, jnp.float32
    dma = pltpu.SemaphoreType.DMA
    vmem = pl.BlockSpec(memory_space=pltpu.VMEM)
    hbm = pl.BlockSpec(memory_space=pl.ANY)
    moved = pl.pallas_call(
        block_kernel,
        out_shape=jax.ShapeDtypeStruct((ROWS, WIDTH), bf16),
        in_specs=[pl.BlockSpec(memory_space=pltpu.SMEM)] + [hbm] * 7,
        out_specs=vmem,
        scratch_shapes=[
            pltpu.SMEM(noise_level.shape, jnp.int32),
            pltpu.VMEM((ROWS, WIDTH), bf16),
            pltpu.VMEM((WIDTH,), f32),
            pltpu.VMEM((WIDTH,), f32),
            pltpu.VMEM((3, D, WIDTH), bf16),
            pltpu.VMEM((WIDTH, D), bf16),
            pltpu.VMEM((3, mod_table.shape[0], D), f32),
            pltpu.VMEM((4, ROWS, WIDTH), bf16),
            pltpu.VMEM((ROWS, D), bf16),
            pltpu.VMEM((2, ROWS, WIDTH), f32),
            pltpu.VMEM((4, 8, 256), f32),
            pltpu.VMEM((3, HEADS_DEV, ROWS, DH), bf16),
            pltpu.VMEM((ZS, ROWS, DH), bf16),
            pltpu.VMEM((2, ZS, ROWS, DH), bf16),
            pltpu.VMEM((2, ZS, ROWS, DH), bf16),
            pltpu.VMEM((ZS, ROWS, DH), bf16),
            pltpu.VMEM((HEADS_DEV, ROWS, DH), bf16),
            pltpu.VMEM((3, ROWS, WIDTH), bf16),
            pltpu.VMEM((3, ROWS, WIDTH), bf16),
            pltpu.VMEM((2, ROWS, 2 * ZS * ROWS), f32),
            pltpu.VMEM((ROWS, WIDTH), bf16),
            dma((7,)),
            dma((3, PIECES)),
            dma((4, PIECES)),
            dma((4,)),
            dma((4,)),
            dma((3, HEADS_DEV)),
            dma((ZS,)),
            dma((2 * ZS,)),
            dma((2 * ZS,)),
            dma((2, ZS)),
            dma((ZS,)),
            dma((HEADS_DEV,)),
            dma((3, PIECES)),
            dma((3, PIECES)),
            dma,
            dma,
        ],
        compiler_params=pltpu.CompilerParams(
            collective_id=0, has_side_effects=True, vmem_limit_bytes=VMEM_BYTES
        ),
    )(
        offset,
        noise_level,
        latents,
        q_gain,
        k_gain,
        jnp.transpose(w_qkv, (1, 0, 2)),
        w_out,
        jnp.transpose(mod_table, (1, 0, 2)),
    )
    my_slab = lax.axis_index("queue")
    entry_slot = jnp.mod(offset[0] - 1, ZS)
    fresh_half = lax.dynamic_slice_in_dim(fresh_frame, my_slab % 2 * ROWS, ROWS, 0)
    return jnp.where(my_slab // 2 == entry_slot, fresh_half, moved)


def solution(mesh):
    fits = mesh.shape["queue"] == 2 * ZS and mesh.shape["head"] == 4
    return jax.shard_map(
        local_fused if fits else local,
        mesh=mesh,
        in_specs=(
            P("queue", "head"),
            P(None, "head"),
            P(),
            P(),
            P(),
            P(None, None, "head"),
            P("head", None),
            P("head"),
            P("head"),
        ),
        out_specs=P("queue", "head"),
        check_vma=False,
    )
```

```python
import math
import jax
import jax.numpy as jnp
from jax import lax
from jax.experimental import pallas as pl
from jax.experimental.pallas import tpu as pltpu
from jax.sharding import PartitionSpec as P

D = 1536
DH = 128


def passed_along(block, axis, distance):
    devices = range(lax.axis_size(axis))
    route = [((i - distance) % len(devices), i) for i in devices]
    return lax.ppermute(block, axis, route)


def attend(carried, queries, key_block, value_block, allowed):
    run_max, run_total, running = carried
    key_count = key_block.shape[0]
    head_count = queries.shape[1]
    key_heads = key_block.reshape(key_count, head_count, DH)
    value_heads = value_block.reshape(key_count, head_count, DH)
    scores = jnp.einsum(
        "qhd,khd->hqk", queries, key_heads, preferred_element_type=jnp.float32
    ) * DH ** (-0.5)
    scores = jnp.where(allowed[None, None, :], scores, -jnp.inf)
    new_max = jnp.maximum(run_max, jnp.max(scores, axis=2))
    rescale = jnp.exp(run_max - new_max)
    exp_scores = jnp.exp(scores - new_max[:, :, None])
    new_total = run_total * rescale + jnp.sum(exp_scores, axis=2)
    added = jnp.einsum(
        "hqk,khd->hqd",
        exp_scores.astype(jnp.bfloat16),
        value_heads,
        preferred_element_type=jnp.float32,
    )
    return (new_max, new_total, running * rescale[:, :, None] + added)


def local(latents, fresh_frame, noise_level, offset, mod_table, w_qkv, w_out, q_gain, k_gain):
    slabs = lax.axis_size("queue")
    frames = slabs // 2
    my_slab = lax.axis_index("queue")
    my_frame = my_slab // 2
    position = jnp.mod(my_frame - offset[0], frames)
    my_level = noise_level[position]
    modulation = lax.dynamic_index_in_dim(mod_table, my_level, 0, keepdims=False)
    whole = lax.all_gather(latents, "head", axis=1, tiled=True).astype(jnp.float32)
    row_count = whole.shape[0]
    centered = whole - jnp.mean(whole, axis=1, keepdims=True)
    variance = jnp.mean(centered * centered, axis=1, keepdims=True)
    normed = centered * lax.rsqrt(variance + 1e-06)
    modded = (normed * (1.0 + modulation[1]) + modulation[0]).astype(jnp.bfloat16)
    local_width = w_qkv.shape[2]
    projected = jnp.dot(
        modded, w_qkv.reshape(w_qkv.shape[0], 3 * local_width), preferred_element_type=jnp.float32
    )
    projected = projected.reshape(row_count, 3, local_width)
    query_raw = projected[:, 0]
    key_raw = projected[:, 1]
    values = projected[:, 2].astype(jnp.bfloat16)
    query_sq, key_sq = lax.psum(
        (jnp.sum(query_raw * query_raw, axis=1), jnp.sum(key_raw * key_raw, axis=1)), "head"
    )
    queries = (query_raw * lax.rsqrt(query_sq / D + 1e-06)[:, None] * q_gain).astype(jnp.bfloat16)
    key_normed = (key_raw * lax.rsqrt(key_sq / D + 1e-06)[:, None] * k_gain).astype(jnp.bfloat16)
    head_count = local_width // DH
    query_heads = queries.reshape(row_count, head_count, DH)
    start_state = (
        jnp.full((head_count, row_count), -1e30, jnp.float32),
        jnp.zeros((head_count, row_count), jnp.float32),
        jnp.zeros((head_count, row_count, DH), jnp.float32),
    )
    all_rows = jnp.ones((row_count,), dtype=bool)
    carried = attend(start_state, query_heads, key_normed, values, all_rows)
    stacked = jnp.stack((key_normed, values))

    def pass_step(turn, loop_state):
        pieces, state_now = loop_state
        pieces = passed_along(pieces, "queue", 1)
        key_slab = jnp.mod(my_slab - turn, slabs)
        key_pos = jnp.mod(key_slab // 2 - offset[0], frames)

        def use_piece(state_in):
            return attend(state_in, query_heads, pieces[0], pieces[1], all_rows)

        def keep_state(state_in):
            return state_in

        state_now = lax.cond(key_pos <= position, use_piece, keep_state, state_now)
        return (pieces, state_now)

    stacked, carried = lax.fori_loop(1, slabs, pass_step, (stacked, carried))
    run_max, run_total, running = carried
    attn = (
        jnp.transpose(running / run_total[:, :, None], (1, 0, 2))
        .reshape(row_count, local_width)
        .astype(jnp.bfloat16)
    )
    partial_out = jnp.dot(attn, w_out, preferred_element_type=jnp.float32)
    proj = lax.psum_scatter(
        partial_out.astype(jnp.bfloat16), "head", scatter_dimension=1, tiled=True
    ).astype(jnp.float32)
    feature_start = lax.axis_index("head") * local_width
    gate_local = lax.dynamic_slice_in_dim(modulation[2], feature_start, local_width)
    updated = (latents.astype(jnp.float32) + gate_local * proj).astype(jnp.bfloat16)
    moved = passed_along(updated, "queue", -2)
    entry_slot = jnp.mod(offset[0] - 1, frames)
    fresh_half = lax.dynamic_slice_in_dim(fresh_frame, my_slab % 2 * row_count, row_count, 0)
    return jnp.where(my_frame == entry_slot, fresh_half, moved)


MESH = pl.DeviceIdType.MESH
ZS = 4
ROWS = 192
WIDTH = 384
HEADS_DEV = 3
PIECES = 2
VMEM_BYTES = 64 * 1024 * 1024 - 128 * 1024
PIECE = ROWS // PIECES


def arrived(buffer, sem):
    pltpu.make_async_copy(buffer, buffer, sem).wait()


def block_kernel(
    offset_ref, noise_hbm, lat_hbm, q_gain_hbm, k_gain_hbm, w_hbm, wout_hbm, mod_hbm, out_ref,
    noise_ref, lat_ref, q_gain, k_gain,
    w_v, wo_v, mod_v, lat_buf, mod_act, raw, stat_buf, stage, q_buf, k_buf, v_buf,
    o_buf, a_buf, w_col, s_buf, lat_next,
    load_sem, lat_send, lat_recv, st_send, st_recv, qkv_send, q_recv, k_recv, v_recv,
    f_send, o_send, o_recv, a_send, w_send, w_recv, mv_send, mv_recv,
):
    queue = lax.axis_index("queue")
    head = lax.axis_index("head")
    z, y = queue // 2, queue % 2
    x, c = head // 2, head % 2
    sib = x * 2 + (1 - c)
    xnb = (1 - x) * 2 + c
    diag = (1 - x) * 2 + (1 - c)
    peers = (head, sib, xnb, diag)
    below = queue - 2 + jnp.where(z == 0, 2 * ZS, 0)
    above = queue + 2 - jnp.where(z == ZS - 1, 2 * ZS, 0)
    swap_head = x * 2 + y
    swap_other = (1 - x) * 2 + y
    on_diagonal = y == c

    def is_self(zt):
        return jnp.logical_and(on_diagonal, zt == z)

    loads = [
        pltpu.make_async_copy(mod_hbm, mod_v, load_sem.at[0]),
        pltpu.make_async_copy(w_hbm, w_v, load_sem.at[1]),
        pltpu.make_async_copy(wout_hbm, wo_v, load_sem.at[2]),
        pltpu.make_async_copy(lat_hbm, lat_ref, load_sem.at[3]),
        pltpu.make_async_copy(noise_hbm, noise_ref, load_sem.at[4]),
        pltpu.make_async_copy(q_gain_hbm, q_gain, load_sem.at[5]),
        pltpu.make_async_copy(k_gain_hbm, k_gain, load_sem.at[6]),
    ]
    for load in loads:
        load.start()

    barrier = pltpu.get_barrier_semaphore()

    def greet(q_id, h_id):
        pl.semaphore_signal(barrier, inc=1, device_id=(q_id, h_id), device_id_type=MESH)

    for peer in peers[1:]:
        greet(queue, peer)
    greet(below, head)
    greet(above, head)
    for zt in range(ZS):
        pl.when(jnp.logical_not(is_self(zt)))(lambda zt=zt: greet(zt * 2 + c, swap_head))
        greet(zt * 2 + c, swap_other)
    pl.semaphore_wait(barrier, 5 + 2 * ZS - jnp.where(on_diagonal, 1, 0))

    def remote(src, dst, s_sem, r_sem, q_id, h_id):
        return pltpu.make_async_remote_copy(
            src_ref=src, dst_ref=dst, send_sem=s_sem, recv_sem=r_sem,
            device_id=(q_id, h_id), device_id_type=MESH,
        )

    loads[3].wait()
    pieces = [pl.ds(p * PIECE, PIECE) for p in range(PIECES)]
    to_x, forward = [], []
    for p, rows in enumerate(pieces):
        to_x.append(remote(
            lat_ref.at[rows], lat_buf.at[2, rows], lat_send.at[0, p], lat_recv.at[2, p], queue, xnb
        ))
        to_x[p].start()
        forward.append(remote(
            lat_buf.at[2, rows], lat_buf.at[3, rows], lat_send.at[2, p], lat_recv.at[3, p], queue, sib
        ))
    to_sib = remote(lat_ref, lat_buf.at[1], lat_send.at[1, 0], lat_recv.at[1, 0], queue, sib)
    to_sib.start()
    lat_move = remote(lat_ref, lat_next, mv_send, mv_recv, below, head)
    lat_move.start()
    for p, rows in enumerate(pieces):
        arrived(lat_buf.at[2, rows], lat_recv.at[2, p])
        forward[p].start()
    arrived(lat_buf.at[1], lat_recv.at[1, 0])
    loads[0].wait()
    for load in loads[4:]:
        load.wait()

    offset = lax.rem(offset_ref[0], ZS)

    def position_of(frame):
        return lax.rem(frame + ZS - offset, ZS)

    level = noise_ref[position_of(z)]
    for p, rows in enumerate(pieces):
        arrived(lat_buf.at[3, rows], lat_recv.at[3, p])

    def block(r):
        return (lat_ref[...] if r == 0 else lat_buf[r]).astype(jnp.float32)

    def columns(r):
        return pl.ds(pl.multiple_of(peers[r] * WIDTH, WIDTH), WIDTH)

    loads[2].wait()
    weights = []

    def send_weights(r, part):
        rows = pl.ds(part * (WIDTH // 2), WIDTH // 2)
        copy = remote(
            wo_v.at[rows, columns(r)], w_col.at[r, rows], w_send.at[r, part], w_recv.at[r, part], queue, peers[r]
        )
        copy.start()
        weights.append(copy)

    send_weights(3, 0)
    mean = sum(jnp.sum(block(r), axis=1, keepdims=True) for r in range(4)) / D
    square = jnp.zeros((ROWS, 1), jnp.float32)
    for r in range(4):
        centered = block(r) - mean
        square += jnp.sum(centered * centered, axis=1, keepdims=True)
    inv = lax.rsqrt(square / D + 1e-06)
    for r in range(4):
        shift = mod_v[0, pl.ds(level, 1), columns(r)]
        scale = mod_v[1, pl.ds(level, 1), columns(r)]
        normed = (block(r) - mean) * inv
        mod_act[:, columns(r)] = (normed * (1.0 + scale) + shift).astype(jnp.bfloat16)

    loads[1].wait()
    sends = []

    def send_part(part, buf, recv_sem):
        for j in range(HEADS_DEV):
            zt = j + c
            mine = is_self(zt)
            src = stage.at[part, j]
            dst = buf.at[z] if part == 0 else buf.at[0, z]
            far = remote(src, dst, qkv_send.at[part, j], recv_sem.at[z], zt * 2 + c, swap_head)
            near = pltpu.make_async_copy(src, dst, recv_sem.at[z])
            pl.when(mine)(near.start)
            pl.when(jnp.logical_not(mine))(far.start)
            sends.append((mine, far))

    values = jnp.dot(mod_act[...], w_v[2], preferred_element_type=jnp.float32)
    for j in range(HEADS_DEV):
        stage[2, j] = values[:, j * DH:(j + 1) * DH].astype(jnp.bfloat16)
    send_part(2, v_buf, v_recv)

    sums = []
    for i in range(2):
        projected = jnp.dot(mod_act[...], w_v[i], preferred_element_type=jnp.float32)
        raw[i] = projected
        sums.append(jnp.sum(projected * projected, axis=1, keepdims=True))
    lane = lax.broadcasted_iota(jnp.int32, (256, 128), 1)
    padding = jnp.zeros((256 - ROWS, 1), jnp.float32)
    spread = jnp.where(
        lane == 0,
        jnp.concatenate([sums[0], padding], axis=0),
        jnp.concatenate([sums[1], padding], axis=0),
    )
    stat_buf[0] = jnp.transpose(spread)[:8]
    stats = [
        remote(stat_buf.at[0], stat_buf.at[r], st_send.at[r], st_recv.at[r], queue, peers[r])
        for r in (2, 3, 1)
    ]
    for copy in stats:
        copy.start()

    for r in (1, 2, 3):
        arrived(stat_buf.at[r], st_recv.at[r])
    total_sq = stat_buf[0] + stat_buf[1] + stat_buf[2] + stat_buf[3]
    rates = lax.rsqrt(total_sq / D + 1e-06)
    rates = jnp.transpose(jnp.concatenate([rates] * 16, axis=0))[:ROWS]
    for part, buf, recv_sem in ((1, k_buf, k_recv), (0, q_buf, q_recv)):
        rate = rates[:, part:part + 1]
        gain = (q_gain, k_gain)[part][...].reshape(1, WIDTH)
        for j in range(HEADS_DEV):
            cols = slice(j * DH, (j + 1) * DH)
            stage[part, j] = (raw[part, :, cols] * rate * gain[:, cols]).astype(jnp.bfloat16)
        send_part(part, buf, recv_sem)

    send_weights(3, 1)
    for r in (2, 1):
        for part in range(2):
            send_weights(r, part)

    active = jnp.logical_and(z - y >= 0, z - y <= 2)
    slot = jnp.where(active, z - y, 0)

    @pl.when(active)
    def _():
        forwards = []
        for kind, (buf, recv_sem) in enumerate(((v_buf, v_recv), (k_buf, k_recv))):
            for s in range(ZS):
                arrived(buf.at[0, s], recv_sem.at[s])
                copy = remote(
                    buf.at[0, s], buf.at[1, s], f_send.at[kind, s], recv_sem.at[ZS + s], queue, sib
                )
                copy.start()
                forwards.append(copy)
        for buf, recv_sem in ((v_buf, v_recv), (k_buf, k_recv)):
            for s in range(ZS):
                arrived(buf.at[1, s], recv_sem.at[ZS + s])
        keys = k_buf[...].reshape(2 * ZS * ROWS, DH)
        vals = v_buf[...].reshape(2 * ZS * ROWS, DH)
        column = lax.broadcasted_iota(jnp.int32, (1, 2 * ZS * ROWS), 1)
        frame = jnp.zeros_like(column)
        for t in range(1, 2 * ZS):
            frame += jnp.where(column >= t * ROWS, 1 if t != ZS else 1 - ZS, 0)
        key_pos = frame - offset
        key_pos = jnp.where(key_pos < 0, key_pos + ZS, key_pos)
        order = (z, z + 1 - 2 * (z % 2), (z + 2) % ZS, ZS - 1 - z)

        def score_into(i):
            arrived(q_buf.at[order[i]], q_recv.at[order[i]])
            s_buf[i % 2] = lax.dot_general(
                q_buf[order[i]], keys, (((1,), (1,)), ((), ())), preferred_element_type=jnp.float32
            )

        outs = []
        score_into(0)
        for i, s in enumerate(order):
            if i + 1 < ZS:
                score_into(i + 1)
            bias = jnp.where(key_pos <= position_of(s), 0.0, -1e30)
            scores = s_buf[i % 2] * (DH ** (-0.5) * math.log2(math.e)) + bias
            top = jnp.max(scores, axis=1, keepdims=True)
            e = jnp.exp2(scores - top)
            total = jnp.sum(e, axis=1, keepdims=True)
            added = jnp.dot(e.astype(jnp.bfloat16), vals, preferred_element_type=jnp.float32)
            o_buf[i] = (added / total).astype(jnp.bfloat16)
            zt = (s + ZS - 1) % ZS
            mine = is_self(zt)
            far = remote(
                o_buf.at[i], a_buf.at[0, slot], o_send.at[0, i], o_recv.at[0, slot], zt * 2 + c, swap_head
            )
            near = pltpu.make_async_copy(o_buf.at[i], a_buf.at[0, slot], o_recv.at[0, slot])
            other = remote(
                o_buf.at[i], a_buf.at[2, slot], o_send.at[1, i], o_recv.at[2, slot], zt * 2 + c, swap_other
            )
            other.start()
            forwards.append(other)
            pl.when(mine)(near.start)
            pl.when(jnp.logical_not(mine))(far.start)
            outs.append((mine, far))
        for copy in forwards:
            copy.wait_send()
        for mine, far in outs:
            pl.when(jnp.logical_not(mine))(far.wait_send)

    shared = []
    for j in range(HEADS_DEV):
        for r in (0, 2):
            arrived(a_buf.at[r, j], o_recv.at[r, j])
            copy = remote(
                a_buf.at[r, j], a_buf.at[r + 1, j], a_send.at[r // 2, j], o_recv.at[r + 1, j], queue, sib
            )
            copy.start()
            shared.append(copy)

    def out_block(r):
        attn = jnp.concatenate([a_buf[r, j] for j in range(HEADS_DEV)], axis=1)
        own = wo_v[:, columns(0)] if r == 0 else w_col[r]
        return jnp.dot(attn, own, preferred_element_type=jnp.float32)

    proj = out_block(0)
    for r in (1, 2, 3):
        for part in range(2):
            rows = pl.ds(part * (WIDTH // 2), WIDTH // 2)
            arrived(w_col.at[r, rows], w_recv.at[r, part])
    proj += out_block(2)
    gate = mod_v[2, pl.ds(noise_ref[position_of((z + 1) % ZS)], 1), columns(0)]
    arrived(lat_next, mv_recv)
    for r in (1, 3):
        for j in range(HEADS_DEV):
            arrived(a_buf.at[r, j], o_recv.at[r, j])
        proj += out_block(r)
    out_ref[...] = (lat_next[...].astype(jnp.float32) + gate * proj).astype(jnp.bfloat16)
    for copy in (*to_x, to_sib, *forward, *stats, *weights, *shared, lat_move):
        copy.wait_send()
    for mine, far in sends:
        pl.when(jnp.logical_not(mine))(far.wait_send)


def local_fused(latents, fresh_frame, noise_level, offset, mod_table, w_qkv, w_out, q_gain, k_gain):
    bf16, f32 = jnp.bfloat16, jnp.float32
    dma = pltpu.SemaphoreType.DMA
    vmem = pl.BlockSpec(memory_space=pltpu.VMEM)
    hbm = pl.BlockSpec(memory_space=pl.ANY)
    moved = pl.pallas_call(
        block_kernel,
        out_shape=jax.ShapeDtypeStruct((ROWS, WIDTH), bf16),
        in_specs=[pl.BlockSpec(memory_space=pltpu.SMEM)] + [hbm] * 7,
        out_specs=vmem,
        scratch_shapes=[
            pltpu.SMEM(noise_level.shape, jnp.int32),
            pltpu.VMEM((ROWS, WIDTH), bf16),
            pltpu.VMEM((WIDTH,), f32),
            pltpu.VMEM((WIDTH,), f32),
            pltpu.VMEM((3, D, WIDTH), bf16),
            pltpu.VMEM((WIDTH, D), bf16),
            pltpu.VMEM((3, mod_table.shape[0], D), f32),
            pltpu.VMEM((4, ROWS, WIDTH), bf16),
            pltpu.VMEM((ROWS, D), bf16),
            pltpu.VMEM((2, ROWS, WIDTH), f32),
            pltpu.VMEM((4, 8, 256), f32),
            pltpu.VMEM((3, HEADS_DEV, ROWS, DH), bf16),
            pltpu.VMEM((ZS, ROWS, DH), bf16),
            pltpu.VMEM((2, ZS, ROWS, DH), bf16),
            pltpu.VMEM((2, ZS, ROWS, DH), bf16),
            pltpu.VMEM((ZS, ROWS, DH), bf16),
            pltpu.VMEM((4, HEADS_DEV, ROWS, DH), bf16),
            pltpu.VMEM((4, WIDTH, WIDTH), bf16),
            pltpu.VMEM((2, ROWS, 2 * ZS * ROWS), f32),
            pltpu.VMEM((ROWS, WIDTH), bf16),
            dma((7,)),
            dma((3, PIECES)),
            dma((4, PIECES)),
            dma((4,)),
            dma((4,)),
            dma((3, HEADS_DEV)),
            dma((ZS,)),
            dma((2 * ZS,)),
            dma((2 * ZS,)),
            dma((2, ZS)),
            dma((2, ZS)),
            dma((4, HEADS_DEV)),
            dma((2, HEADS_DEV)),
            dma((4, 2)),
            dma((4, 2)),
            dma,
            dma,
        ],
        compiler_params=pltpu.CompilerParams(
            collective_id=0, has_side_effects=True, vmem_limit_bytes=VMEM_BYTES
        ),
    )(
        offset,
        noise_level,
        latents,
        q_gain,
        k_gain,
        jnp.transpose(w_qkv, (1, 0, 2)),
        w_out,
        jnp.transpose(mod_table, (1, 0, 2)),
    )
    my_slab = lax.axis_index("queue")
    entry_slot = jnp.mod(offset[0] - 1, ZS)
    fresh_half = lax.dynamic_slice_in_dim(fresh_frame, my_slab % 2 * ROWS, ROWS, 0)
    return jnp.where(my_slab // 2 == entry_slot, fresh_half, moved)


def solution(mesh):
    fits = mesh.shape["queue"] == 2 * ZS and mesh.shape["head"] == 4
    return jax.shard_map(
        local_fused if fits else local,
        mesh=mesh,
        in_specs=(
            P("queue", "head"),
            P(None, "head"),
            P(),
            P(),
            P(),
            P(None, None, "head"),
            P("head", None),
            P("head"),
            P("head"),
        ),
        out_specs=P("queue", "head"),
        check_vma=False,
    )
```

```python
import math
import jax
import jax.numpy as jnp
from jax import lax
from jax.experimental import pallas as pl
from jax.experimental.pallas import tpu as pltpu
from jax.sharding import PartitionSpec as P

D = 1536
DH = 128


def passed_along(block, axis, distance):
    devices = range(lax.axis_size(axis))
    route = [((i - distance) % len(devices), i) for i in devices]
    return lax.ppermute(block, axis, route)


def attend(carried, queries, key_block, value_block, allowed):
    run_max, run_total, running = carried
    key_count = key_block.shape[0]
    head_count = queries.shape[1]
    key_heads = key_block.reshape(key_count, head_count, DH)
    value_heads = value_block.reshape(key_count, head_count, DH)
    scores = jnp.einsum(
        "qhd,khd->hqk", queries, key_heads, preferred_element_type=jnp.float32
    ) * DH ** (-0.5)
    scores = jnp.where(allowed[None, None, :], scores, -jnp.inf)
    new_max = jnp.maximum(run_max, jnp.max(scores, axis=2))
    rescale = jnp.exp(run_max - new_max)
    exp_scores = jnp.exp(scores - new_max[:, :, None])
    new_total = run_total * rescale + jnp.sum(exp_scores, axis=2)
    added = jnp.einsum(
        "hqk,khd->hqd",
        exp_scores.astype(jnp.bfloat16),
        value_heads,
        preferred_element_type=jnp.float32,
    )
    return (new_max, new_total, running * rescale[:, :, None] + added)


def local(latents, fresh_frame, noise_level, offset, mod_table, w_qkv, w_out, q_gain, k_gain):
    slabs = lax.axis_size("queue")
    frames = slabs // 2
    my_slab = lax.axis_index("queue")
    my_frame = my_slab // 2
    position = jnp.mod(my_frame - offset[0], frames)
    my_level = noise_level[position]
    modulation = lax.dynamic_index_in_dim(mod_table, my_level, 0, keepdims=False)
    whole = lax.all_gather(latents, "head", axis=1, tiled=True).astype(jnp.float32)
    row_count = whole.shape[0]
    centered = whole - jnp.mean(whole, axis=1, keepdims=True)
    variance = jnp.mean(centered * centered, axis=1, keepdims=True)
    normed = centered * lax.rsqrt(variance + 1e-06)
    modded = (normed * (1.0 + modulation[1]) + modulation[0]).astype(jnp.bfloat16)
    local_width = w_qkv.shape[2]
    projected = jnp.dot(
        modded, w_qkv.reshape(w_qkv.shape[0], 3 * local_width), preferred_element_type=jnp.float32
    )
    projected = projected.reshape(row_count, 3, local_width)
    query_raw = projected[:, 0]
    key_raw = projected[:, 1]
    values = projected[:, 2].astype(jnp.bfloat16)
    query_sq, key_sq = lax.psum(
        (jnp.sum(query_raw * query_raw, axis=1), jnp.sum(key_raw * key_raw, axis=1)), "head"
    )
    queries = (query_raw * lax.rsqrt(query_sq / D + 1e-06)[:, None] * q_gain).astype(jnp.bfloat16)
    key_normed = (key_raw * lax.rsqrt(key_sq / D + 1e-06)[:, None] * k_gain).astype(jnp.bfloat16)
    head_count = local_width // DH
    query_heads = queries.reshape(row_count, head_count, DH)
    start_state = (
        jnp.full((head_count, row_count), -1e30, jnp.float32),
        jnp.zeros((head_count, row_count), jnp.float32),
        jnp.zeros((head_count, row_count, DH), jnp.float32),
    )
    all_rows = jnp.ones((row_count,), dtype=bool)
    carried = attend(start_state, query_heads, key_normed, values, all_rows)
    stacked = jnp.stack((key_normed, values))

    def pass_step(turn, loop_state):
        pieces, state_now = loop_state
        pieces = passed_along(pieces, "queue", 1)
        key_slab = jnp.mod(my_slab - turn, slabs)
        key_pos = jnp.mod(key_slab // 2 - offset[0], frames)

        def use_piece(state_in):
            return attend(state_in, query_heads, pieces[0], pieces[1], all_rows)

        def keep_state(state_in):
            return state_in

        state_now = lax.cond(key_pos <= position, use_piece, keep_state, state_now)
        return (pieces, state_now)

    stacked, carried = lax.fori_loop(1, slabs, pass_step, (stacked, carried))
    run_max, run_total, running = carried
    attn = (
        jnp.transpose(running / run_total[:, :, None], (1, 0, 2))
        .reshape(row_count, local_width)
        .astype(jnp.bfloat16)
    )
    partial_out = jnp.dot(attn, w_out, preferred_element_type=jnp.float32)
    proj = lax.psum_scatter(
        partial_out.astype(jnp.bfloat16), "head", scatter_dimension=1, tiled=True
    ).astype(jnp.float32)
    feature_start = lax.axis_index("head") * local_width
    gate_local = lax.dynamic_slice_in_dim(modulation[2], feature_start, local_width)
    updated = (latents.astype(jnp.float32) + gate_local * proj).astype(jnp.bfloat16)
    moved = passed_along(updated, "queue", -2)
    entry_slot = jnp.mod(offset[0] - 1, frames)
    fresh_half = lax.dynamic_slice_in_dim(fresh_frame, my_slab % 2 * row_count, row_count, 0)
    return jnp.where(my_frame == entry_slot, fresh_half, moved)


MESH = pl.DeviceIdType.MESH
ZS = 4
ROWS = 192
WIDTH = 384
HEADS_DEV = 3
PIECES = 2
VMEM_BYTES = 64 * 1024 * 1024 - 128 * 1024
PIECE = ROWS // PIECES


def arrived(buffer, sem):
    pltpu.make_async_copy(buffer, buffer, sem).wait()


def block_kernel(
    offset_ref, noise_hbm, lat_hbm, q_gain_hbm, k_gain_hbm, w_hbm, wout_hbm, mod_hbm, out_ref,
    noise_ref, lat_ref, q_gain, k_gain,
    w_v, wo_v, mod_v, lat_buf, mod_act, raw, stat_buf, stage, q_buf, k_buf, v_buf,
    o_buf, a_buf, p_send, rs_buf, s_buf, lat_next,
    load_sem, lat_send, lat_recv, st_send, st_recv, qkv_send, q_recv, k_recv, v_recv,
    f_send, o_send, o_recv, rs_send, rs_recv, mv_send, mv_recv,
):
    queue = lax.axis_index("queue")
    head = lax.axis_index("head")
    z, y = queue // 2, queue % 2
    x, c = head // 2, head % 2
    sib = x * 2 + (1 - c)
    xnb = (1 - x) * 2 + c
    diag = (1 - x) * 2 + (1 - c)
    peers = (head, sib, xnb, diag)
    below = queue - 2 + jnp.where(z == 0, 2 * ZS, 0)
    above = queue + 2 - jnp.where(z == ZS - 1, 2 * ZS, 0)
    swap_head = x * 2 + y
    on_diagonal = y == c

    def is_self(zt):
        return jnp.logical_and(on_diagonal, zt == z)

    loads = [
        pltpu.make_async_copy(mod_hbm, mod_v, load_sem.at[0]),
        pltpu.make_async_copy(w_hbm, w_v, load_sem.at[1]),
        pltpu.make_async_copy(wout_hbm, wo_v, load_sem.at[2]),
        pltpu.make_async_copy(lat_hbm, lat_ref, load_sem.at[3]),
        pltpu.make_async_copy(noise_hbm, noise_ref, load_sem.at[4]),
        pltpu.make_async_copy(q_gain_hbm, q_gain, load_sem.at[5]),
        pltpu.make_async_copy(k_gain_hbm, k_gain, load_sem.at[6]),
    ]
    for load in loads:
        load.start()

    barrier = pltpu.get_barrier_semaphore()

    def greet(q_id, h_id):
        pl.semaphore_signal(barrier, inc=1, device_id=(q_id, h_id), device_id_type=MESH)

    for peer in peers[1:]:
        greet(queue, peer)
    greet(below, head)
    greet(above, head)
    for zt in range(ZS):
        pl.when(jnp.logical_not(is_self(zt)))(lambda zt=zt: greet(zt * 2 + c, swap_head))
    pl.semaphore_wait(barrier, 5 + ZS - jnp.where(on_diagonal, 1, 0))

    def remote(src, dst, s_sem, r_sem, q_id, h_id):
        return pltpu.make_async_remote_copy(
            src_ref=src, dst_ref=dst, send_sem=s_sem, recv_sem=r_sem,
            device_id=(q_id, h_id), device_id_type=MESH,
        )

    loads[3].wait()
    pieces = [pl.ds(p * PIECE, PIECE) for p in range(PIECES)]
    to_x, to_sib, forward, stats, sends = [], [], [], [], []
    for p, rows in enumerate(pieces):
        to_x.append(remote(
            lat_ref.at[rows], lat_buf.at[2, rows], lat_send.at[0, p], lat_recv.at[2, p], queue, xnb
        ))
        to_x[p].start()
    for p, rows in enumerate(pieces):
        to_sib.append(remote(
            lat_ref.at[rows], lat_buf.at[1, rows], lat_send.at[1, p], lat_recv.at[1, p], queue, sib
        ))
        to_sib[p].start()
        forward.append(remote(
            lat_buf.at[2, rows], lat_buf.at[3, rows], lat_send.at[2, p], lat_recv.at[3, p], queue, sib
        ))

    def pass_latents(p):
        arrived(lat_buf.at[2, pieces[p]], lat_recv.at[2, p])
        forward[p].start()

    pass_latents(0)
    lat_move = remote(lat_ref, lat_next, mv_send, mv_recv, below, head)
    lat_move.start()
    loads[0].wait()
    for load in loads[4:]:
        load.wait()

    offset = lax.rem(offset_ref[0], ZS)

    def position_of(frame):
        return lax.rem(frame + ZS - offset, ZS)

    level = noise_ref[position_of(z)]

    def columns(r):
        return pl.ds(pl.multiple_of(peers[r] * WIDTH, WIDTH), WIDTH)

    def norm_piece(p):
        rows = pieces[p]
        for r in (1, 3):
            arrived(lat_buf.at[r, rows], lat_recv.at[r, p])

        def block(r):
            return (lat_ref[rows] if r == 0 else lat_buf[r, rows]).astype(jnp.float32)

        mean = sum(jnp.sum(block(r), axis=1, keepdims=True) for r in range(4)) / D
        square = jnp.zeros((PIECE, 1), jnp.float32)
        for r in range(4):
            centered = block(r) - mean
            square += jnp.sum(centered * centered, axis=1, keepdims=True)
        inv = lax.rsqrt(square / D + 1e-06)
        for r in range(4):
            shift = mod_v[0, pl.ds(level, 1), columns(r)]
            scale = mod_v[1, pl.ds(level, 1), columns(r)]
            normed = (block(r) - mean) * inv
            mod_act[rows, columns(r)] = (normed * (1.0 + scale) + shift).astype(jnp.bfloat16)

    def send_part(part, p, buf, recv_sem):
        rows = pieces[p]
        for j in range(HEADS_DEV):
            zt = j + c
            mine = is_self(zt)
            src = stage.at[part, j, rows]
            dst = buf.at[z, rows] if part == 0 else buf.at[0, z, rows]
            far = remote(src, dst, qkv_send.at[part, j, p], recv_sem.at[z], zt * 2 + c, swap_head)
            near = pltpu.make_async_copy(src, dst, recv_sem.at[z])
            pl.when(mine)(near.start)
            pl.when(jnp.logical_not(mine))(far.start)
            sends.append((mine, far))

    def project_values(p):
        rows = pieces[p]
        values = jnp.dot(mod_act[rows], w_v[2], preferred_element_type=jnp.float32)
        for j in range(HEADS_DEV):
            stage[2, j, rows] = values[:, j * DH:(j + 1) * DH].astype(jnp.bfloat16)
        send_part(2, p, v_buf, v_recv)

    def project_keys(p):
        rows = pieces[p]
        sums = []
        for i in range(2):
            projected = jnp.dot(mod_act[rows], w_v[i], preferred_element_type=jnp.float32)
            raw[i, rows] = projected
            sums.append(jnp.sum(projected * projected, axis=1, keepdims=True))
        lane = lax.broadcasted_iota(jnp.int32, (128, 128), 1)
        padding = jnp.zeros((128 - PIECE, 1), jnp.float32)
        spread = jnp.where(
            lane == 0,
            jnp.concatenate([sums[0], padding], axis=0),
            jnp.concatenate([sums[1], padding], axis=0),
        )
        stat_buf[p, 0] = jnp.transpose(spread)[:8]
        for r in (2, 3, 1):
            copy = remote(
                stat_buf.at[p, 0], stat_buf.at[p, r], st_send.at[p, r], st_recv.at[p, r], queue, peers[r]
            )
            copy.start()
            stats.append(copy)

    def send_keys(p):
        rows = pieces[p]
        for r in (1, 2, 3):
            arrived(stat_buf.at[p, r], st_recv.at[p, r])
        total_sq = stat_buf[p, 0] + stat_buf[p, 1] + stat_buf[p, 2] + stat_buf[p, 3]
        rates = lax.rsqrt(total_sq / D + 1e-06)
        rates = jnp.transpose(jnp.concatenate([rates] * 16, axis=0))[:PIECE]
        for part, buf, recv_sem in ((1, k_buf, k_recv), (0, q_buf, q_recv)):
            rate = rates[:, part:part + 1]
            gain = (q_gain, k_gain)[part][...].reshape(1, WIDTH)
            for j in range(HEADS_DEV):
                cols = slice(j * DH, (j + 1) * DH)
                stage[part, j, rows] = (raw[part, rows, cols] * rate * gain[:, cols]).astype(jnp.bfloat16)
            send_part(part, p, buf, recv_sem)

    norm_piece(0)
    loads[1].wait()
    project_values(0)
    pass_latents(1)
    project_keys(0)
    norm_piece(1)
    project_values(1)
    project_keys(1)
    send_keys(0)
    send_keys(1)

    active = jnp.logical_and(z - y >= 0, z - y <= 2)
    slot = jnp.where(active, z - y, 0)

    @pl.when(active)
    def _():
        forwards = []
        for kind, (buf, recv_sem) in enumerate(((v_buf, v_recv), (k_buf, k_recv))):
            for s in range(ZS):
                arrived(buf.at[0, s], recv_sem.at[s])
                copy = remote(
                    buf.at[0, s], buf.at[1, s], f_send.at[kind, s], recv_sem.at[ZS + s], queue, sib
                )
                copy.start()
                forwards.append(copy)
        for buf, recv_sem in ((v_buf, v_recv), (k_buf, k_recv)):
            for s in range(ZS):
                arrived(buf.at[1, s], recv_sem.at[ZS + s])
        keys = k_buf[...].reshape(2 * ZS * ROWS, DH)
        vals = v_buf[...].reshape(2 * ZS * ROWS, DH)
        column = lax.broadcasted_iota(jnp.int32, (1, 2 * ZS * ROWS), 1)
        frame = jnp.zeros_like(column)
        for t in range(1, 2 * ZS):
            frame += jnp.where(column >= t * ROWS, 1 if t != ZS else 1 - ZS, 0)
        key_pos = frame - offset
        key_pos = jnp.where(key_pos < 0, key_pos + ZS, key_pos)
        order = (z, z + 1 - 2 * (z % 2), (z + 2) % ZS, ZS - 1 - z)

        def score_into(i):
            arrived(q_buf.at[order[i]], q_recv.at[order[i]])
            s_buf[i % 2] = lax.dot_general(
                q_buf[order[i]], keys, (((1,), (1,)), ((), ())), preferred_element_type=jnp.float32
            )

        outs = []
        score_into(0)
        for i, s in enumerate(order):
            if i + 1 < ZS:
                score_into(i + 1)
            bias = jnp.where(key_pos <= position_of(s), 0.0, -1e30)
            scores = s_buf[i % 2] * (DH ** (-0.5) * math.log2(math.e)) + bias
            top = jnp.max(scores, axis=1, keepdims=True)
            e = jnp.exp2(scores - top)
            total = jnp.sum(e, axis=1, keepdims=True)
            added = jnp.dot(e.astype(jnp.bfloat16), vals, preferred_element_type=jnp.float32)
            o_buf[i] = (added / total).astype(jnp.bfloat16)
            zt = (s + ZS - 1) % ZS
            mine = is_self(zt)
            far = remote(
                o_buf.at[i], a_buf.at[slot], o_send.at[i], o_recv.at[slot], zt * 2 + c, swap_head
            )
            near = pltpu.make_async_copy(o_buf.at[i], a_buf.at[slot], o_recv.at[slot])
            pl.when(mine)(near.start)
            pl.when(jnp.logical_not(mine))(far.start)
            outs.append((mine, far))
        for copy in forwards:
            copy.wait_send()
        for mine, far in outs:
            pl.when(jnp.logical_not(mine))(far.wait_send)

    loads[2].wait()
    for j in range(HEADS_DEV):
        arrived(a_buf.at[j], o_recv.at[j])
    attn = jnp.concatenate([a_buf[j] for j in range(HEADS_DEV)], axis=1)

    def out_block(r):
        return jnp.dot(attn, wo_v[:, columns(r)], preferred_element_type=jnp.float32)

    def rs_copy(kind, p, q_id, h_id):
        rows = pieces[p]
        return remote(
            p_send.at[kind, rows], rs_buf.at[kind, rows], rs_send.at[kind, p], rs_recv.at[kind, p], q_id, h_id
        )

    send_a, send_b, send_c = [], [], []
    p_send[0] = out_block(3).astype(jnp.bfloat16)
    for p in range(PIECES):
        send_a.append(rs_copy(0, p, queue, sib))
        send_a[p].start()
    ahead = out_block(2)
    p_send[1] = out_block(1).astype(jnp.bfloat16)
    for p in range(PIECES):
        send_b.append(rs_copy(1, p, queue, sib))
        send_b[p].start()
    for p, rows in enumerate(pieces):
        arrived(rs_buf.at[0, rows], rs_recv.at[0, p])
        mine = ahead[p * PIECE:(p + 1) * PIECE]
        p_send[2, rows] = (mine + rs_buf[0, rows].astype(jnp.float32)).astype(jnp.bfloat16)
        send_c.append(rs_copy(2, p, queue, xnb))
        send_c[p].start()
    proj = out_block(0)
    gate = mod_v[2, pl.ds(noise_ref[position_of((z + 1) % ZS)], 1), columns(0)]
    arrived(lat_next, mv_recv)
    for p, rows in enumerate(pieces):
        arrived(rs_buf.at[1, rows], rs_recv.at[1, p])
    proj += rs_buf[1].astype(jnp.float32)
    for p, rows in enumerate(pieces):
        arrived(rs_buf.at[2, rows], rs_recv.at[2, p])
        full = proj[p * PIECE:(p + 1) * PIECE] + rs_buf[2, rows].astype(jnp.float32)
        out_ref[rows] = (lat_next[rows].astype(jnp.float32) + gate * full).astype(jnp.bfloat16)
    for copy in (*to_x, *to_sib, *forward, *stats, *send_a, *send_b, *send_c, lat_move):
        copy.wait_send()
    for mine, far in sends:
        pl.when(jnp.logical_not(mine))(far.wait_send)


def local_fused(latents, fresh_frame, noise_level, offset, mod_table, w_qkv, w_out, q_gain, k_gain):
    bf16, f32 = jnp.bfloat16, jnp.float32
    dma = pltpu.SemaphoreType.DMA
    vmem = pl.BlockSpec(memory_space=pltpu.VMEM)
    hbm = pl.BlockSpec(memory_space=pl.ANY)
    moved = pl.pallas_call(
        block_kernel,
        out_shape=jax.ShapeDtypeStruct((ROWS, WIDTH), bf16),
        in_specs=[pl.BlockSpec(memory_space=pltpu.SMEM)] + [hbm] * 7,
        out_specs=vmem,
        scratch_shapes=[
            pltpu.SMEM(noise_level.shape, jnp.int32),
            pltpu.VMEM((ROWS, WIDTH), bf16),
            pltpu.VMEM((WIDTH,), f32),
            pltpu.VMEM((WIDTH,), f32),
            pltpu.VMEM((3, D, WIDTH), bf16),
            pltpu.VMEM((WIDTH, D), bf16),
            pltpu.VMEM((3, mod_table.shape[0], D), f32),
            pltpu.VMEM((4, ROWS, WIDTH), bf16),
            pltpu.VMEM((ROWS, D), bf16),
            pltpu.VMEM((2, ROWS, WIDTH), f32),
            pltpu.VMEM((PIECES, 4, 8, 128), f32),
            pltpu.VMEM((3, HEADS_DEV, ROWS, DH), bf16),
            pltpu.VMEM((ZS, ROWS, DH), bf16),
            pltpu.VMEM((2, ZS, ROWS, DH), bf16),
            pltpu.VMEM((2, ZS, ROWS, DH), bf16),
            pltpu.VMEM((ZS, ROWS, DH), bf16),
            pltpu.VMEM((HEADS_DEV, ROWS, DH), bf16),
            pltpu.VMEM((3, ROWS, WIDTH), bf16),
            pltpu.VMEM((3, ROWS, WIDTH), bf16),
            pltpu.VMEM((2, ROWS, 2 * ZS * ROWS), f32),
            pltpu.VMEM((ROWS, WIDTH), bf16),
            dma((7,)),
            dma((3, PIECES)),
            dma((4, PIECES)),
            dma((PIECES, 4)),
            dma((PIECES, 4)),
            dma((3, HEADS_DEV, PIECES)),
            dma((ZS,)),
            dma((2 * ZS,)),
            dma((2 * ZS,)),
            dma((2, ZS)),
            dma((ZS,)),
            dma((HEADS_DEV,)),
            dma((3, PIECES)),
            dma((3, PIECES)),
            dma,
            dma,
        ],
        compiler_params=pltpu.CompilerParams(
            collective_id=0, has_side_effects=True, vmem_limit_bytes=VMEM_BYTES
        ),
    )(
        offset,
        noise_level,
        latents,
        q_gain,
        k_gain,
        jnp.transpose(w_qkv, (1, 0, 2)),
        w_out,
        jnp.transpose(mod_table, (1, 0, 2)),
    )
    my_slab = lax.axis_index("queue")
    entry_slot = jnp.mod(offset[0] - 1, ZS)
    fresh_half = lax.dynamic_slice_in_dim(fresh_frame, my_slab % 2 * ROWS, ROWS, 0)
    return jnp.where(my_slab // 2 == entry_slot, fresh_half, moved)


def solution(mesh):
    fits = mesh.shape["queue"] == 2 * ZS and mesh.shape["head"] == 4
    return jax.shard_map(
        local_fused if fits else local,
        mesh=mesh,
        in_specs=(
            P("queue", "head"),
            P(None, "head"),
            P(),
            P(),
            P(),
            P(None, None, "head"),
            P("head", None),
            P("head"),
            P("head"),
        ),
        out_specs=P("queue", "head"),
        check_vma=False,
    )
```

```python
import math
import jax
import jax.numpy as jnp
from jax import lax
from jax.experimental import pallas as pl
from jax.experimental.pallas import tpu as pltpu
from jax.sharding import PartitionSpec as P

D = 1536
DH = 128


def passed_along(block, axis, distance):
    devices = range(lax.axis_size(axis))
    route = [((i - distance) % len(devices), i) for i in devices]
    return lax.ppermute(block, axis, route)


def attend(carried, queries, key_block, value_block, allowed):
    run_max, run_total, running = carried
    key_count = key_block.shape[0]
    head_count = queries.shape[1]
    key_heads = key_block.reshape(key_count, head_count, DH)
    value_heads = value_block.reshape(key_count, head_count, DH)
    scores = jnp.einsum(
        "qhd,khd->hqk", queries, key_heads, preferred_element_type=jnp.float32
    ) * DH ** (-0.5)
    scores = jnp.where(allowed[None, None, :], scores, -jnp.inf)
    new_max = jnp.maximum(run_max, jnp.max(scores, axis=2))
    rescale = jnp.exp(run_max - new_max)
    exp_scores = jnp.exp(scores - new_max[:, :, None])
    new_total = run_total * rescale + jnp.sum(exp_scores, axis=2)
    added = jnp.einsum(
        "hqk,khd->hqd",
        exp_scores.astype(jnp.bfloat16),
        value_heads,
        preferred_element_type=jnp.float32,
    )
    return (new_max, new_total, running * rescale[:, :, None] + added)


def local(latents, fresh_frame, noise_level, offset, mod_table, w_qkv, w_out, q_gain, k_gain):
    slabs = lax.axis_size("queue")
    frames = slabs // 2
    my_slab = lax.axis_index("queue")
    my_frame = my_slab // 2
    position = jnp.mod(my_frame - offset[0], frames)
    my_level = noise_level[position]
    modulation = lax.dynamic_index_in_dim(mod_table, my_level, 0, keepdims=False)
    whole = lax.all_gather(latents, "head", axis=1, tiled=True).astype(jnp.float32)
    row_count = whole.shape[0]
    centered = whole - jnp.mean(whole, axis=1, keepdims=True)
    variance = jnp.mean(centered * centered, axis=1, keepdims=True)
    normed = centered * lax.rsqrt(variance + 1e-06)
    modded = (normed * (1.0 + modulation[1]) + modulation[0]).astype(jnp.bfloat16)
    local_width = w_qkv.shape[2]
    projected = jnp.dot(
        modded, w_qkv.reshape(w_qkv.shape[0], 3 * local_width), preferred_element_type=jnp.float32
    )
    projected = projected.reshape(row_count, 3, local_width)
    query_raw = projected[:, 0]
    key_raw = projected[:, 1]
    values = projected[:, 2].astype(jnp.bfloat16)
    query_sq, key_sq = lax.psum(
        (jnp.sum(query_raw * query_raw, axis=1), jnp.sum(key_raw * key_raw, axis=1)), "head"
    )
    queries = (query_raw * lax.rsqrt(query_sq / D + 1e-06)[:, None] * q_gain).astype(jnp.bfloat16)
    key_normed = (key_raw * lax.rsqrt(key_sq / D + 1e-06)[:, None] * k_gain).astype(jnp.bfloat16)
    head_count = local_width // DH
    query_heads = queries.reshape(row_count, head_count, DH)
    start_state = (
        jnp.full((head_count, row_count), -1e30, jnp.float32),
        jnp.zeros((head_count, row_count), jnp.float32),
        jnp.zeros((head_count, row_count, DH), jnp.float32),
    )
    all_rows = jnp.ones((row_count,), dtype=bool)
    carried = attend(start_state, query_heads, key_normed, values, all_rows)
    stacked = jnp.stack((key_normed, values))

    def pass_step(turn, loop_state):
        pieces, state_now = loop_state
        pieces = passed_along(pieces, "queue", 1)
        key_slab = jnp.mod(my_slab - turn, slabs)
        key_pos = jnp.mod(key_slab // 2 - offset[0], frames)

        def use_piece(state_in):
            return attend(state_in, query_heads, pieces[0], pieces[1], all_rows)

        def keep_state(state_in):
            return state_in

        state_now = lax.cond(key_pos <= position, use_piece, keep_state, state_now)
        return (pieces, state_now)

    stacked, carried = lax.fori_loop(1, slabs, pass_step, (stacked, carried))
    run_max, run_total, running = carried
    attn = (
        jnp.transpose(running / run_total[:, :, None], (1, 0, 2))
        .reshape(row_count, local_width)
        .astype(jnp.bfloat16)
    )
    partial_out = jnp.dot(attn, w_out, preferred_element_type=jnp.float32)
    proj = lax.psum_scatter(
        partial_out.astype(jnp.bfloat16), "head", scatter_dimension=1, tiled=True
    ).astype(jnp.float32)
    feature_start = lax.axis_index("head") * local_width
    gate_local = lax.dynamic_slice_in_dim(modulation[2], feature_start, local_width)
    updated = (latents.astype(jnp.float32) + gate_local * proj).astype(jnp.bfloat16)
    moved = passed_along(updated, "queue", -2)
    entry_slot = jnp.mod(offset[0] - 1, frames)
    fresh_half = lax.dynamic_slice_in_dim(fresh_frame, my_slab % 2 * row_count, row_count, 0)
    return jnp.where(my_frame == entry_slot, fresh_half, moved)


MESH = pl.DeviceIdType.MESH
ZS = 4
ROWS = 192
WIDTH = 384
HEADS_DEV = 3
PIECES = 2
VMEM_BYTES = 64 * 1024 * 1024 - 128 * 1024
PIECE = ROWS // PIECES


def arrived(buffer, sem):
    pltpu.make_async_copy(buffer, buffer, sem).wait()


def block_kernel(
    offset_ref, noise_hbm, lat_hbm, q_gain_hbm, k_gain_hbm, w_hbm, wout_hbm, mod_hbm, out_ref,
    noise_ref, lat_ref, q_gain, k_gain,
    w_v, wo_v, mod_v, lat_buf, mod_act, raw, stat_buf, stage_kq, stage_v, kq_buf, v_buf, k_sib, v_sib,
    o_buf, a_buf, p_send, rs_buf, s_buf, lat_next,
    load_sem, lat_send, lat_recv, st_send, st_recv, qkv_send, kq_recv, v_recv, ks_recv, vs_recv,
    f_send, o_send, o_recv, rs_send, rs_recv, mv_send, mv_recv,
):
    queue = lax.axis_index("queue")
    head = lax.axis_index("head")
    z, y = queue // 2, queue % 2
    x, c = head // 2, head % 2
    sib = x * 2 + (1 - c)
    xnb = (1 - x) * 2 + c
    diag = (1 - x) * 2 + (1 - c)
    peers = (head, sib, xnb, diag)
    below = queue - 2 + jnp.where(z == 0, 2 * ZS, 0)
    above = queue + 2 - jnp.where(z == ZS - 1, 2 * ZS, 0)
    swap_head = x * 2 + y
    on_diagonal = y == c

    def is_self(zt):
        return jnp.logical_and(on_diagonal, zt == z)

    loads = [
        pltpu.make_async_copy(mod_hbm, mod_v, load_sem.at[0]),
        pltpu.make_async_copy(w_hbm, w_v, load_sem.at[1]),
        pltpu.make_async_copy(wout_hbm, wo_v, load_sem.at[2]),
        pltpu.make_async_copy(lat_hbm, lat_ref, load_sem.at[3]),
        pltpu.make_async_copy(noise_hbm, noise_ref, load_sem.at[4]),
        pltpu.make_async_copy(q_gain_hbm, q_gain, load_sem.at[5]),
        pltpu.make_async_copy(k_gain_hbm, k_gain, load_sem.at[6]),
    ]
    for load in loads:
        load.start()

    barrier = pltpu.get_barrier_semaphore()

    def greet(q_id, h_id):
        pl.semaphore_signal(barrier, inc=1, device_id=(q_id, h_id), device_id_type=MESH)

    for peer in peers[1:]:
        greet(queue, peer)
    greet(below, head)
    greet(above, head)
    for zt in range(ZS):
        pl.when(jnp.logical_not(is_self(zt)))(lambda zt=zt: greet(zt * 2 + c, swap_head))
    pl.semaphore_wait(barrier, 5 + ZS - jnp.where(on_diagonal, 1, 0))

    def remote(src, dst, s_sem, r_sem, q_id, h_id):
        return pltpu.make_async_remote_copy(
            src_ref=src, dst_ref=dst, send_sem=s_sem, recv_sem=r_sem,
            device_id=(q_id, h_id), device_id_type=MESH,
        )

    loads[3].wait()
    pieces = [pl.ds(p * PIECE, PIECE) for p in range(PIECES)]
    to_x = remote(lat_ref, lat_buf.at[2], lat_send.at[0], lat_recv.at[2], queue, xnb)
    to_x.start()
    to_sib = remote(lat_ref, lat_buf.at[1], lat_send.at[1], lat_recv.at[1], queue, sib)
    to_sib.start()
    lat_move = remote(lat_ref, lat_next, mv_send, mv_recv, below, head)
    lat_move.start()
    forward = remote(lat_buf.at[2], lat_buf.at[3], lat_send.at[2], lat_recv.at[3], queue, sib)
    arrived(lat_buf.at[2], lat_recv.at[2])
    forward.start()
    arrived(lat_buf.at[1], lat_recv.at[1])
    loads[0].wait()
    for load in loads[4:]:
        load.wait()

    offset = lax.rem(offset_ref[0], ZS)

    def position_of(frame):
        return lax.rem(frame + ZS - offset, ZS)

    level = noise_ref[position_of(z)]
    arrived(lat_buf.at[3], lat_recv.at[3])

    def block(r):
        return (lat_ref[...] if r == 0 else lat_buf[r]).astype(jnp.float32)

    def columns(r):
        return pl.ds(pl.multiple_of(peers[r] * WIDTH, WIDTH), WIDTH)

    mean = sum(jnp.sum(block(r), axis=1, keepdims=True) for r in range(4)) / D
    square = jnp.zeros((ROWS, 1), jnp.float32)
    for r in range(4):
        centered = block(r) - mean
        square += jnp.sum(centered * centered, axis=1, keepdims=True)
    inv = lax.rsqrt(square / D + 1e-06)
    for r in range(4):
        shift = mod_v[0, pl.ds(level, 1), columns(r)]
        scale = mod_v[1, pl.ds(level, 1), columns(r)]
        normed = (block(r) - mean) * inv
        mod_act[:, columns(r)] = (normed * (1.0 + scale) + shift).astype(jnp.bfloat16)

    loads[1].wait()
    sends = []

    def send_part(part, buf, recv_sem):
        for j in range(HEADS_DEV):
            zt = j + c
            mine = is_self(zt)
            src = stage_v.at[j] if part == 2 else stage_kq.at[j]
            far = remote(src, buf.at[z], qkv_send.at[part, j], recv_sem.at[z], zt * 2 + c, swap_head)
            near = pltpu.make_async_copy(src, buf.at[z], recv_sem.at[z])
            pl.when(mine)(near.start)
            pl.when(jnp.logical_not(mine))(far.start)
            sends.append((mine, far))

    values = jnp.dot(mod_act[...], w_v[2], preferred_element_type=jnp.float32)
    for j in range(HEADS_DEV):
        stage_v[j] = values[:, j * DH:(j + 1) * DH].astype(jnp.bfloat16)
    send_part(2, v_buf, v_recv)

    sums = []
    for i in range(2):
        projected = jnp.dot(mod_act[...], w_v[i], preferred_element_type=jnp.float32)
        raw[i] = projected
        sums.append(jnp.sum(projected * projected, axis=1, keepdims=True))
    lane = lax.broadcasted_iota(jnp.int32, (256, 128), 1)
    padding = jnp.zeros((256 - ROWS, 1), jnp.float32)
    spread = jnp.where(
        lane == 0,
        jnp.concatenate([sums[0], padding], axis=0),
        jnp.concatenate([sums[1], padding], axis=0),
    )
    stat_buf[0] = jnp.transpose(spread)[:8]
    stats = [
        remote(stat_buf.at[0], stat_buf.at[r], st_send.at[r], st_recv.at[r], queue, peers[r])
        for r in (2, 3, 1)
    ]
    for copy in stats:
        copy.start()

    for r in (1, 2, 3):
        arrived(stat_buf.at[r], st_recv.at[r])
    total_sq = stat_buf[0] + stat_buf[1] + stat_buf[2] + stat_buf[3]
    rates = lax.rsqrt(total_sq / D + 1e-06)
    rates = jnp.transpose(jnp.concatenate([rates] * 16, axis=0))[:ROWS]
    for part in range(2):
        rate = rates[:, part:part + 1]
        gain = (q_gain, k_gain)[part][...].reshape(1, WIDTH)
        for j in range(HEADS_DEV):
            cols = slice(j * DH, (j + 1) * DH)
            stage_kq[j, part] = (raw[part, :, cols] * rate * gain[:, cols]).astype(jnp.bfloat16)
    send_part(1, kq_buf, kq_recv)

    active = jnp.logical_and(z - y >= 0, z - y <= 2)
    slot = jnp.where(active, z - y, 0)

    @pl.when(active)
    def _():
        order = (z, z + 1 - 2 * (z % 2), (z + 2) % ZS, ZS - 1 - z)
        for s in range(ZS):
            arrived(v_buf.at[s], v_recv.at[s])
        pass_values = remote(v_buf, v_sib, f_send.at[ZS], vs_recv, queue, sib)
        pass_values.start()
        forwards = [pass_values]
        for s in order:
            arrived(kq_buf.at[s], kq_recv.at[s])
            copy = remote(kq_buf.at[s, 1], k_sib.at[s], f_send.at[s], ks_recv.at[s], queue, sib)
            copy.start()
            forwards.append(copy)
        arrived(v_sib, vs_recv)
        for s in range(ZS):
            arrived(k_sib.at[s], ks_recv.at[s])
        keys = jnp.concatenate(
            [kq_buf[s, 1] for s in range(ZS)] + [k_sib[s] for s in range(ZS)], axis=0
        )
        vals = jnp.concatenate(
            [v_buf[s] for s in range(ZS)] + [v_sib[s] for s in range(ZS)], axis=0
        )
        column = lax.broadcasted_iota(jnp.int32, (1, 2 * ZS * ROWS), 1)
        frame = jnp.zeros_like(column)
        for t in range(1, 2 * ZS):
            frame += jnp.where(column >= t * ROWS, 1 if t != ZS else 1 - ZS, 0)
        key_pos = frame - offset
        key_pos = jnp.where(key_pos < 0, key_pos + ZS, key_pos)

        def score_into(i):
            s_buf[i % 2] = lax.dot_general(
                kq_buf[order[i], 0], keys, (((1,), (1,)), ((), ())), preferred_element_type=jnp.float32
            )

        outs = []
        score_into(0)
        for i, s in enumerate(order):
            if i + 1 < ZS:
                score_into(i + 1)
            bias = jnp.where(key_pos <= position_of(s), 0.0, -1e30)
            scores = s_buf[i % 2] * (DH ** (-0.5) * math.log2(math.e)) + bias
            top = jnp.max(scores, axis=1, keepdims=True)
            e = jnp.exp2(scores - top)
            total = jnp.sum(e, axis=1, keepdims=True)
            added = jnp.dot(e.astype(jnp.bfloat16), vals, preferred_element_type=jnp.float32)
            o_buf[i] = (added / total).astype(jnp.bfloat16)
            zt = (s + ZS - 1) % ZS
            mine = is_self(zt)
            far = remote(
                o_buf.at[i], a_buf.at[slot], o_send.at[i], o_recv.at[slot], zt * 2 + c, swap_head
            )
            near = pltpu.make_async_copy(o_buf.at[i], a_buf.at[slot], o_recv.at[slot])
            pl.when(mine)(near.start)
            pl.when(jnp.logical_not(mine))(far.start)
            outs.append((mine, far))
        for copy in forwards:
            copy.wait_send()
        for mine, far in outs:
            pl.when(jnp.logical_not(mine))(far.wait_send)

    loads[2].wait()
    for j in range(HEADS_DEV):
        arrived(a_buf.at[j], o_recv.at[j])
    attn = jnp.concatenate([a_buf[j] for j in range(HEADS_DEV)], axis=1)

    def out_block(r):
        return jnp.dot(attn, wo_v[:, columns(r)], preferred_element_type=jnp.float32)

    def rs_copy(kind, p, q_id, h_id):
        rows = pieces[p]
        return remote(
            p_send.at[kind, rows], rs_buf.at[kind, rows], rs_send.at[kind, p], rs_recv.at[kind, p], q_id, h_id
        )

    send_c = []
    p_send[0] = out_block(3).astype(jnp.bfloat16)
    send_a = remote(p_send.at[0], rs_buf.at[0], rs_send.at[0, 0], rs_recv.at[0, 0], queue, sib)
    send_a.start()
    ahead = out_block(2)
    p_send[1] = out_block(1).astype(jnp.bfloat16)
    send_b = remote(p_send.at[1], rs_buf.at[1], rs_send.at[1, 0], rs_recv.at[1, 0], queue, sib)
    send_b.start()
    arrived(rs_buf.at[0], rs_recv.at[0, 0])
    for p, rows in enumerate(pieces):
        mine = ahead[p * PIECE:(p + 1) * PIECE]
        p_send[2, rows] = (mine + rs_buf[0, rows].astype(jnp.float32)).astype(jnp.bfloat16)
        send_c.append(rs_copy(2, p, queue, xnb))
        send_c[p].start()
    proj = out_block(0)
    gate = mod_v[2, pl.ds(noise_ref[position_of((z + 1) % ZS)], 1), columns(0)]
    arrived(lat_next, mv_recv)
    arrived(rs_buf.at[1], rs_recv.at[1, 0])
    proj += rs_buf[1].astype(jnp.float32)
    for p, rows in enumerate(pieces):
        arrived(rs_buf.at[2, rows], rs_recv.at[2, p])
        full = proj[p * PIECE:(p + 1) * PIECE] + rs_buf[2, rows].astype(jnp.float32)
        out_ref[rows] = (lat_next[rows].astype(jnp.float32) + gate * full).astype(jnp.bfloat16)
    for copy in (to_x, to_sib, forward, *stats, send_a, send_b, *send_c, lat_move):
        copy.wait_send()
    for mine, far in sends:
        pl.when(jnp.logical_not(mine))(far.wait_send)


def local_fused(latents, fresh_frame, noise_level, offset, mod_table, w_qkv, w_out, q_gain, k_gain):
    bf16, f32 = jnp.bfloat16, jnp.float32
    dma = pltpu.SemaphoreType.DMA
    vmem = pl.BlockSpec(memory_space=pltpu.VMEM)
    hbm = pl.BlockSpec(memory_space=pl.ANY)
    moved = pl.pallas_call(
        block_kernel,
        out_shape=jax.ShapeDtypeStruct((ROWS, WIDTH), bf16),
        in_specs=[pl.BlockSpec(memory_space=pltpu.SMEM)] + [hbm] * 7,
        out_specs=vmem,
        scratch_shapes=[
            pltpu.SMEM(noise_level.shape, jnp.int32),
            pltpu.VMEM((ROWS, WIDTH), bf16),
            pltpu.VMEM((WIDTH,), f32),
            pltpu.VMEM((WIDTH,), f32),
            pltpu.VMEM((3, D, WIDTH), bf16),
            pltpu.VMEM((WIDTH, D), bf16),
            pltpu.VMEM((3, mod_table.shape[0], D), f32),
            pltpu.VMEM((4, ROWS, WIDTH), bf16),
            pltpu.VMEM((ROWS, D), bf16),
            pltpu.VMEM((2, ROWS, WIDTH), f32),
            pltpu.VMEM((4, 8, 256), f32),
            pltpu.VMEM((HEADS_DEV, 2, ROWS, DH), bf16),
            pltpu.VMEM((HEADS_DEV, ROWS, DH), bf16),
            pltpu.VMEM((ZS, 2, ROWS, DH), bf16),
            pltpu.VMEM((ZS, ROWS, DH), bf16),
            pltpu.VMEM((ZS, ROWS, DH), bf16),
            pltpu.VMEM((ZS, ROWS, DH), bf16),
            pltpu.VMEM((ZS, ROWS, DH), bf16),
            pltpu.VMEM((HEADS_DEV, ROWS, DH), bf16),
            pltpu.VMEM((3, ROWS, WIDTH), bf16),
            pltpu.VMEM((3, ROWS, WIDTH), bf16),
            pltpu.VMEM((2, ROWS, 2 * ZS * ROWS), f32),
            pltpu.VMEM((ROWS, WIDTH), bf16),
            dma((7,)),
            dma((3,)),
            dma((4,)),
            dma((4,)),
            dma((4,)),
            dma((3, HEADS_DEV)),
            dma((ZS,)),
            dma((ZS,)),
            dma((ZS,)),
            dma,
            dma((ZS + 1,)),
            dma((ZS,)),
            dma((HEADS_DEV,)),
            dma((3, PIECES)),
            dma((3, PIECES)),
            dma,
            dma,
        ],
        compiler_params=pltpu.CompilerParams(
            collective_id=0, has_side_effects=True, vmem_limit_bytes=VMEM_BYTES
        ),
    )(
        offset,
        noise_level,
        latents,
        q_gain,
        k_gain,
        jnp.transpose(w_qkv, (1, 0, 2)),
        w_out,
        jnp.transpose(mod_table, (1, 0, 2)),
    )
    my_slab = lax.axis_index("queue")
    entry_slot = jnp.mod(offset[0] - 1, ZS)
    fresh_half = lax.dynamic_slice_in_dim(fresh_frame, my_slab % 2 * ROWS, ROWS, 0)
    return jnp.where(my_slab // 2 == entry_slot, fresh_half, moved)


def solution(mesh):
    fits = mesh.shape["queue"] == 2 * ZS and mesh.shape["head"] == 4
    return jax.shard_map(
        local_fused if fits else local,
        mesh=mesh,
        in_specs=(
            P("queue", "head"),
            P(None, "head"),
            P(),
            P(),
            P(),
            P(None, None, "head"),
            P("head", None),
            P("head"),
            P("head"),
        ),
        out_specs=P("queue", "head"),
        check_vma=False,
    )
```

```python
import math
import jax
import jax.numpy as jnp
from jax import lax
from jax.experimental import pallas as pl
from jax.experimental.pallas import tpu as pltpu
from jax.sharding import PartitionSpec as P

D = 1536
DH = 128


def passed_along(block, axis, distance):
    devices = range(lax.axis_size(axis))
    route = [((i - distance) % len(devices), i) for i in devices]
    return lax.ppermute(block, axis, route)


def attend(carried, queries, key_block, value_block, allowed):
    run_max, run_total, running = carried
    key_count = key_block.shape[0]
    head_count = queries.shape[1]
    key_heads = key_block.reshape(key_count, head_count, DH)
    value_heads = value_block.reshape(key_count, head_count, DH)
    scores = jnp.einsum(
        "qhd,khd->hqk", queries, key_heads, preferred_element_type=jnp.float32
    ) * DH ** (-0.5)
    scores = jnp.where(allowed[None, None, :], scores, -jnp.inf)
    new_max = jnp.maximum(run_max, jnp.max(scores, axis=2))
    rescale = jnp.exp(run_max - new_max)
    exp_scores = jnp.exp(scores - new_max[:, :, None])
    new_total = run_total * rescale + jnp.sum(exp_scores, axis=2)
    added = jnp.einsum(
        "hqk,khd->hqd",
        exp_scores.astype(jnp.bfloat16),
        value_heads,
        preferred_element_type=jnp.float32,
    )
    return (new_max, new_total, running * rescale[:, :, None] + added)


def local(latents, fresh_frame, noise_level, offset, mod_table, w_qkv, w_out, q_gain, k_gain):
    slabs = lax.axis_size("queue")
    frames = slabs // 2
    my_slab = lax.axis_index("queue")
    my_frame = my_slab // 2
    position = jnp.mod(my_frame - offset[0], frames)
    my_level = noise_level[position]
    modulation = lax.dynamic_index_in_dim(mod_table, my_level, 0, keepdims=False)
    whole = lax.all_gather(latents, "head", axis=1, tiled=True).astype(jnp.float32)
    row_count = whole.shape[0]
    centered = whole - jnp.mean(whole, axis=1, keepdims=True)
    variance = jnp.mean(centered * centered, axis=1, keepdims=True)
    normed = centered * lax.rsqrt(variance + 1e-06)
    modded = (normed * (1.0 + modulation[1]) + modulation[0]).astype(jnp.bfloat16)
    local_width = w_qkv.shape[2]
    projected = jnp.dot(
        modded, w_qkv.reshape(w_qkv.shape[0], 3 * local_width), preferred_element_type=jnp.float32
    )
    projected = projected.reshape(row_count, 3, local_width)
    query_raw = projected[:, 0]
    key_raw = projected[:, 1]
    values = projected[:, 2].astype(jnp.bfloat16)
    query_sq, key_sq = lax.psum(
        (jnp.sum(query_raw * query_raw, axis=1), jnp.sum(key_raw * key_raw, axis=1)), "head"
    )
    queries = (query_raw * lax.rsqrt(query_sq / D + 1e-06)[:, None] * q_gain).astype(jnp.bfloat16)
    key_normed = (key_raw * lax.rsqrt(key_sq / D + 1e-06)[:, None] * k_gain).astype(jnp.bfloat16)
    head_count = local_width // DH
    query_heads = queries.reshape(row_count, head_count, DH)
    start_state = (
        jnp.full((head_count, row_count), -1e30, jnp.float32),
        jnp.zeros((head_count, row_count), jnp.float32),
        jnp.zeros((head_count, row_count, DH), jnp.float32),
    )
    all_rows = jnp.ones((row_count,), dtype=bool)
    carried = attend(start_state, query_heads, key_normed, values, all_rows)
    stacked = jnp.stack((key_normed, values))

    def pass_step(turn, loop_state):
        pieces, state_now = loop_state
        pieces = passed_along(pieces, "queue", 1)
        key_slab = jnp.mod(my_slab - turn, slabs)
        key_pos = jnp.mod(key_slab // 2 - offset[0], frames)

        def use_piece(state_in):
            return attend(state_in, query_heads, pieces[0], pieces[1], all_rows)

        def keep_state(state_in):
            return state_in

        state_now = lax.cond(key_pos <= position, use_piece, keep_state, state_now)
        return (pieces, state_now)

    stacked, carried = lax.fori_loop(1, slabs, pass_step, (stacked, carried))
    run_max, run_total, running = carried
    attn = (
        jnp.transpose(running / run_total[:, :, None], (1, 0, 2))
        .reshape(row_count, local_width)
        .astype(jnp.bfloat16)
    )
    partial_out = jnp.dot(attn, w_out, preferred_element_type=jnp.float32)
    proj = lax.psum_scatter(
        partial_out.astype(jnp.bfloat16), "head", scatter_dimension=1, tiled=True
    ).astype(jnp.float32)
    feature_start = lax.axis_index("head") * local_width
    gate_local = lax.dynamic_slice_in_dim(modulation[2], feature_start, local_width)
    updated = (latents.astype(jnp.float32) + gate_local * proj).astype(jnp.bfloat16)
    moved = passed_along(updated, "queue", -2)
    entry_slot = jnp.mod(offset[0] - 1, frames)
    fresh_half = lax.dynamic_slice_in_dim(fresh_frame, my_slab % 2 * row_count, row_count, 0)
    return jnp.where(my_frame == entry_slot, fresh_half, moved)


MESH = pl.DeviceIdType.MESH
ZS = 4
ROWS = 192
WIDTH = 384
HEADS_DEV = 3
PIECES = 3
VMEM_BYTES = 64 * 1024 * 1024 - 128 * 1024
PIECE = ROWS // PIECES


def arrived(buffer, sem):
    pltpu.make_async_copy(buffer, buffer, sem).wait()


def block_kernel(
    offset_ref, noise_hbm, lat_hbm, q_gain_hbm, k_gain_hbm, w_hbm, wout_hbm, mod_hbm, out_ref,
    noise_ref, lat_ref, q_gain, k_gain,
    w_v, wo_v, mod_v, lat_buf, mod_act, raw, stat_buf, stage, q_buf, k_buf, v_buf,
    o_buf, a_buf, p_send, rs_buf, s_buf, lat_next,
    load_sem, lat_send, lat_recv, st_send, st_recv, qkv_send, q_recv, k_recv, v_recv,
    f_send, o_send, o_recv, rs_send, rs_recv, mv_send, mv_recv,
):
    queue = lax.axis_index("queue")
    head = lax.axis_index("head")
    z, y = queue // 2, queue % 2
    x, c = head // 2, head % 2
    sib = x * 2 + (1 - c)
    xnb = (1 - x) * 2 + c
    diag = (1 - x) * 2 + (1 - c)
    peers = (head, sib, xnb, diag)
    below = queue - 2 + jnp.where(z == 0, 2 * ZS, 0)
    above = queue + 2 - jnp.where(z == ZS - 1, 2 * ZS, 0)
    swap_head = x * 2 + y
    on_diagonal = y == c
    order = (ZS - 1 - z, (z + 2) % ZS, z + 1 - 2 * (z % 2), z)

    def is_self(zt):
        return jnp.logical_and(on_diagonal, zt == z)

    loads = [
        pltpu.make_async_copy(mod_hbm, mod_v, load_sem.at[0]),
        pltpu.make_async_copy(w_hbm, w_v, load_sem.at[1]),
        pltpu.make_async_copy(wout_hbm, wo_v, load_sem.at[2]),
        pltpu.make_async_copy(lat_hbm, lat_ref, load_sem.at[3]),
        pltpu.make_async_copy(noise_hbm, noise_ref, load_sem.at[4]),
        pltpu.make_async_copy(q_gain_hbm, q_gain, load_sem.at[5]),
        pltpu.make_async_copy(k_gain_hbm, k_gain, load_sem.at[6]),
    ]
    for load in loads:
        load.start()

    barrier = pltpu.get_barrier_semaphore()

    def greet(q_id, h_id):
        pl.semaphore_signal(barrier, inc=1, device_id=(q_id, h_id), device_id_type=MESH)

    for peer in peers[1:]:
        greet(queue, peer)
    greet(below, head)
    greet(above, head)
    for zt in range(ZS):
        pl.when(jnp.logical_not(is_self(zt)))(lambda zt=zt: greet(zt * 2 + c, swap_head))
    pl.semaphore_wait(barrier, 5 + ZS - jnp.where(on_diagonal, 1, 0))

    def remote(src, dst, s_sem, r_sem, q_id, h_id):
        return pltpu.make_async_remote_copy(
            src_ref=src, dst_ref=dst, send_sem=s_sem, recv_sem=r_sem,
            device_id=(q_id, h_id), device_id_type=MESH,
        )

    loads[3].wait()
    pieces = [pl.ds(p * PIECE, PIECE) for p in range(PIECES)]
    to_x, forward = [], []
    for p, rows in enumerate(pieces):
        to_x.append(remote(
            lat_ref.at[rows], lat_buf.at[2, rows], lat_send.at[0, p], lat_recv.at[2, p], queue, xnb
        ))
        to_x[p].start()
        forward.append(remote(
            lat_buf.at[2, rows], lat_buf.at[3, rows], lat_send.at[2, p], lat_recv.at[3, p], queue, sib
        ))
    to_sib = remote(lat_ref, lat_buf.at[1], lat_send.at[1, 0], lat_recv.at[1, 0], queue, sib)
    to_sib.start()
    lat_move = remote(lat_ref, lat_next, mv_send, mv_recv, below, head)
    lat_move.start()
    for p, rows in enumerate(pieces):
        arrived(lat_buf.at[2, rows], lat_recv.at[2, p])
        forward[p].start()
    arrived(lat_buf.at[1], lat_recv.at[1, 0])
    loads[0].wait()
    for load in loads[4:]:
        load.wait()

    offset = lax.rem(offset_ref[0], ZS)

    def position_of(frame):
        return lax.rem(frame + ZS - offset, ZS)

    level = noise_ref[position_of(z)]
    for p, rows in enumerate(pieces):
        arrived(lat_buf.at[3, rows], lat_recv.at[3, p])

    def block(r):
        return (lat_ref[...] if r == 0 else lat_buf[r]).astype(jnp.float32)

    def columns(r):
        return pl.ds(pl.multiple_of(peers[r] * WIDTH, WIDTH), WIDTH)

    mean = sum(jnp.sum(block(r), axis=1, keepdims=True) for r in range(4)) / D
    square = jnp.zeros((ROWS, 1), jnp.float32)
    for r in range(4):
        centered = block(r) - mean
        square += jnp.sum(centered * centered, axis=1, keepdims=True)
    inv = lax.rsqrt(square / D + 1e-06)
    for r in range(4):
        shift = mod_v[0, pl.ds(level, 1), columns(r)]
        scale = mod_v[1, pl.ds(level, 1), columns(r)]
        normed = (block(r) - mean) * inv
        mod_act[:, columns(r)] = (normed * (1.0 + scale) + shift).astype(jnp.bfloat16)

    loads[1].wait()
    sends = []

    def send_part(part, buf, recv_sem):
        for i, zt in enumerate(order):
            valid = jnp.logical_and(zt - c >= 0, zt - c < HEADS_DEV)
            src = stage.at[part, jnp.where(valid, zt - c, 0)]
            dst = buf.at[z] if part == 0 else buf.at[0, z]
            far = remote(src, dst, qkv_send.at[part, i], recv_sem.at[z], zt * 2 + c, swap_head)
            away = valid
            if i == ZS - 1:
                near = pltpu.make_async_copy(src, dst, recv_sem.at[z])
                pl.when(jnp.logical_and(valid, on_diagonal))(near.start)
                away = jnp.logical_and(valid, jnp.logical_not(on_diagonal))
            pl.when(away)(far.start)
            sends.append((away, far))

    values = jnp.dot(mod_act[...], w_v[2], preferred_element_type=jnp.float32)
    for j in range(HEADS_DEV):
        stage[2, j] = values[:, j * DH:(j + 1) * DH].astype(jnp.bfloat16)
    send_part(2, v_buf, v_recv)

    sums = []
    for i in range(2):
        projected = jnp.dot(mod_act[...], w_v[i], preferred_element_type=jnp.float32)
        raw[i] = projected
        sums.append(jnp.sum(projected * projected, axis=1, keepdims=True))
    lane = lax.broadcasted_iota(jnp.int32, (256, 128), 1)
    padding = jnp.zeros((256 - ROWS, 1), jnp.float32)
    spread = jnp.where(
        lane == 0,
        jnp.concatenate([sums[0], padding], axis=0),
        jnp.concatenate([sums[1], padding], axis=0),
    )
    stat_buf[0] = jnp.transpose(spread)[:8]
    stats = [
        remote(stat_buf.at[0], stat_buf.at[r], st_send.at[r], st_recv.at[r], queue, peers[r])
        for r in (2, 3, 1)
    ]
    for copy in stats:
        copy.start()

    for r in (1, 2, 3):
        arrived(stat_buf.at[r], st_recv.at[r])
    total_sq = stat_buf[0] + stat_buf[1] + stat_buf[2] + stat_buf[3]
    rates = lax.rsqrt(total_sq / D + 1e-06)
    rates = jnp.transpose(jnp.concatenate([rates] * 16, axis=0))[:ROWS]
    for part, buf, recv_sem in ((1, k_buf, k_recv), (0, q_buf, q_recv)):
        rate = rates[:, part:part + 1]
        gain = (q_gain, k_gain)[part][...].reshape(1, WIDTH)
        for j in range(HEADS_DEV):
            cols = slice(j * DH, (j + 1) * DH)
            stage[part, j] = (raw[part, :, cols] * rate * gain[:, cols]).astype(jnp.bfloat16)
        send_part(part, buf, recv_sem)

    active = jnp.logical_and(z - y >= 0, z - y <= 2)
    slot = jnp.where(active, z - y, 0)

    @pl.when(active)
    def _():
        forwards = []
        for kind, (buf, recv_sem) in enumerate(((v_buf, v_recv), (k_buf, k_recv))):
            for i, s in enumerate(order):
                arrived(buf.at[0, s], recv_sem.at[s])
                copy = remote(
                    buf.at[0, s], buf.at[1, s], f_send.at[kind, i], recv_sem.at[ZS + s], queue, sib
                )
                copy.start()
                forwards.append(copy)
        for buf, recv_sem in ((v_buf, v_recv), (k_buf, k_recv)):
            for s in range(ZS):
                arrived(buf.at[1, s], recv_sem.at[ZS + s])
        keys = k_buf[...].reshape(2 * ZS * ROWS, DH)
        vals = v_buf[...].reshape(2 * ZS * ROWS, DH)
        column = lax.broadcasted_iota(jnp.int32, (1, 2 * ZS * ROWS), 1)
        frame = jnp.zeros_like(column)
        for t in range(1, 2 * ZS):
            frame += jnp.where(column >= t * ROWS, 1 if t != ZS else 1 - ZS, 0)
        key_pos = frame - offset
        key_pos = jnp.where(key_pos < 0, key_pos + ZS, key_pos)
        def score_into(i):
            arrived(q_buf.at[order[i]], q_recv.at[order[i]])
            s_buf[i % 2] = lax.dot_general(
                q_buf[order[i]], keys, (((1,), (1,)), ((), ())), preferred_element_type=jnp.float32
            )

        outs = []
        score_into(0)
        for i, s in enumerate(order):
            if i + 1 < ZS:
                score_into(i + 1)
            bias = jnp.where(key_pos <= position_of(s), 0.0, -1e30)
            scores = s_buf[i % 2] * (DH ** (-0.5) * math.log2(math.e)) + bias
            top = jnp.max(scores, axis=1, keepdims=True)
            e = jnp.exp2(scores - top)
            total = jnp.sum(e, axis=1, keepdims=True)
            added = jnp.dot(e.astype(jnp.bfloat16), vals, preferred_element_type=jnp.float32)
            o_buf[i] = (added / total).astype(jnp.bfloat16)
            zt = (s + ZS - 1) % ZS
            mine = is_self(zt)
            far = remote(
                o_buf.at[i], a_buf.at[slot], o_send.at[i], o_recv.at[slot], zt * 2 + c, swap_head
            )
            near = pltpu.make_async_copy(o_buf.at[i], a_buf.at[slot], o_recv.at[slot])
            pl.when(mine)(near.start)
            pl.when(jnp.logical_not(mine))(far.start)
            outs.append((mine, far))
        for copy in forwards:
            copy.wait_send()
        for mine, far in outs:
            pl.when(jnp.logical_not(mine))(far.wait_send)

    loads[2].wait()
    for j in range(HEADS_DEV):
        arrived(a_buf.at[j], o_recv.at[j])
    attn = jnp.concatenate([a_buf[j] for j in range(HEADS_DEV)], axis=1)

    def out_block(r):
        return jnp.dot(attn, wo_v[:, columns(r)], preferred_element_type=jnp.float32)

    def rs_copy(kind, p, q_id, h_id):
        rows = pieces[p]
        return remote(
            p_send.at[kind, rows], rs_buf.at[kind, rows], rs_send.at[kind, p], rs_recv.at[kind, p], q_id, h_id
        )

    send_a, send_b, send_c = [], [], []
    p_send[0] = out_block(3).astype(jnp.bfloat16)
    for p in range(PIECES):
        send_a.append(rs_copy(0, p, queue, sib))
        send_a[p].start()
    ahead = out_block(2)
    p_send[1] = out_block(1).astype(jnp.bfloat16)
    for p in range(PIECES):
        send_b.append(rs_copy(1, p, queue, sib))
        send_b[p].start()
    for p, rows in enumerate(pieces):
        arrived(rs_buf.at[0, rows], rs_recv.at[0, p])
        mine = ahead[p * PIECE:(p + 1) * PIECE]
        p_send[2, rows] = (mine + rs_buf[0, rows].astype(jnp.float32)).astype(jnp.bfloat16)
        send_c.append(rs_copy(2, p, queue, xnb))
        send_c[p].start()
    proj = out_block(0)
    gate = mod_v[2, pl.ds(noise_ref[position_of((z + 1) % ZS)], 1), columns(0)]
    arrived(lat_next, mv_recv)
    for p, rows in enumerate(pieces):
        arrived(rs_buf.at[1, rows], rs_recv.at[1, p])
    proj += rs_buf[1].astype(jnp.float32)
    for p, rows in enumerate(pieces):
        arrived(rs_buf.at[2, rows], rs_recv.at[2, p])
        full = proj[p * PIECE:(p + 1) * PIECE] + rs_buf[2, rows].astype(jnp.float32)
        out_ref[rows] = (lat_next[rows].astype(jnp.float32) + gate * full).astype(jnp.bfloat16)
    for copy in (*to_x, to_sib, *forward, *stats, *send_a, *send_b, *send_c, lat_move):
        copy.wait_send()
    for away, far in sends:
        pl.when(away)(far.wait_send)


def local_fused(latents, fresh_frame, noise_level, offset, mod_table, w_qkv, w_out, q_gain, k_gain):
    bf16, f32 = jnp.bfloat16, jnp.float32
    dma = pltpu.SemaphoreType.DMA
    vmem = pl.BlockSpec(memory_space=pltpu.VMEM)
    hbm = pl.BlockSpec(memory_space=pl.ANY)
    moved = pl.pallas_call(
        block_kernel,
        out_shape=jax.ShapeDtypeStruct((ROWS, WIDTH), bf16),
        in_specs=[pl.BlockSpec(memory_space=pltpu.SMEM)] + [hbm] * 7,
        out_specs=vmem,
        scratch_shapes=[
            pltpu.SMEM(noise_level.shape, jnp.int32),
            pltpu.VMEM((ROWS, WIDTH), bf16),
            pltpu.VMEM((WIDTH,), f32),
            pltpu.VMEM((WIDTH,), f32),
            pltpu.VMEM((3, D, WIDTH), bf16),
            pltpu.VMEM((WIDTH, D), bf16),
            pltpu.VMEM((3, mod_table.shape[0], D), f32),
            pltpu.VMEM((4, ROWS, WIDTH), bf16),
            pltpu.VMEM((ROWS, D), bf16),
            pltpu.VMEM((2, ROWS, WIDTH), f32),
            pltpu.VMEM((4, 8, 256), f32),
            pltpu.VMEM((3, HEADS_DEV, ROWS, DH), bf16),
            pltpu.VMEM((ZS, ROWS, DH), bf16),
            pltpu.VMEM((2, ZS, ROWS, DH), bf16),
            pltpu.VMEM((2, ZS, ROWS, DH), bf16),
            pltpu.VMEM((ZS, ROWS, DH), bf16),
            pltpu.VMEM((HEADS_DEV, ROWS, DH), bf16),
            pltpu.VMEM((3, ROWS, WIDTH), bf16),
            pltpu.VMEM((3, ROWS, WIDTH), bf16),
            pltpu.VMEM((2, ROWS, 2 * ZS * ROWS), f32),
            pltpu.VMEM((ROWS, WIDTH), bf16),
            dma((7,)),
            dma((3, PIECES)),
            dma((4, PIECES)),
            dma((4,)),
            dma((4,)),
            dma((3, ZS)),
            dma((ZS,)),
            dma((2 * ZS,)),
            dma((2 * ZS,)),
            dma((2, ZS)),
            dma((ZS,)),
            dma((HEADS_DEV,)),
            dma((3, PIECES)),
            dma((3, PIECES)),
            dma,
            dma,
        ],
        compiler_params=pltpu.CompilerParams(
            collective_id=0, has_side_effects=True, vmem_limit_bytes=VMEM_BYTES
        ),
    )(
        offset,
        noise_level,
        latents,
        q_gain,
        k_gain,
        jnp.transpose(w_qkv, (1, 0, 2)),
        w_out,
        jnp.transpose(mod_table, (1, 0, 2)),
    )
    my_slab = lax.axis_index("queue")
    entry_slot = jnp.mod(offset[0] - 1, ZS)
    fresh_half = lax.dynamic_slice_in_dim(fresh_frame, my_slab % 2 * ROWS, ROWS, 0)
    return jnp.where(my_slab // 2 == entry_slot, fresh_half, moved)


def solution(mesh):
    fits = mesh.shape["queue"] == 2 * ZS and mesh.shape["head"] == 4
    return jax.shard_map(
        local_fused if fits else local,
        mesh=mesh,
        in_specs=(
            P("queue", "head"),
            P(None, "head"),
            P(),
            P(),
            P(),
            P(None, None, "head"),
            P("head", None),
            P("head"),
            P("head"),
        ),
        out_specs=P("queue", "head"),
        check_vma=False,
    )
```

```python
import math
import jax
import jax.numpy as jnp
from jax import lax
from jax.experimental import pallas as pl
from jax.experimental.pallas import tpu as pltpu
from jax.sharding import PartitionSpec as P

D = 1536
DH = 128


def passed_along(block, axis, distance):
    devices = range(lax.axis_size(axis))
    route = [((i - distance) % len(devices), i) for i in devices]
    return lax.ppermute(block, axis, route)


def attend(carried, queries, key_block, value_block, allowed):
    run_max, run_total, running = carried
    key_count = key_block.shape[0]
    head_count = queries.shape[1]
    key_heads = key_block.reshape(key_count, head_count, DH)
    value_heads = value_block.reshape(key_count, head_count, DH)
    scores = jnp.einsum(
        "qhd,khd->hqk", queries, key_heads, preferred_element_type=jnp.float32
    ) * DH ** (-0.5)
    scores = jnp.where(allowed[None, None, :], scores, -jnp.inf)
    new_max = jnp.maximum(run_max, jnp.max(scores, axis=2))
    rescale = jnp.exp(run_max - new_max)
    exp_scores = jnp.exp(scores - new_max[:, :, None])
    new_total = run_total * rescale + jnp.sum(exp_scores, axis=2)
    added = jnp.einsum(
        "hqk,khd->hqd",
        exp_scores.astype(jnp.bfloat16),
        value_heads,
        preferred_element_type=jnp.float32,
    )
    return (new_max, new_total, running * rescale[:, :, None] + added)


def local(latents, fresh_frame, noise_level, offset, mod_table, w_qkv, w_out, q_gain, k_gain):
    slabs = lax.axis_size("queue")
    frames = slabs // 2
    my_slab = lax.axis_index("queue")
    my_frame = my_slab // 2
    position = jnp.mod(my_frame - offset[0], frames)
    my_level = noise_level[position]
    modulation = lax.dynamic_index_in_dim(mod_table, my_level, 0, keepdims=False)
    whole = lax.all_gather(latents, "head", axis=1, tiled=True).astype(jnp.float32)
    row_count = whole.shape[0]
    centered = whole - jnp.mean(whole, axis=1, keepdims=True)
    variance = jnp.mean(centered * centered, axis=1, keepdims=True)
    normed = centered * lax.rsqrt(variance + 1e-06)
    modded = (normed * (1.0 + modulation[1]) + modulation[0]).astype(jnp.bfloat16)
    local_width = w_qkv.shape[2]
    projected = jnp.dot(
        modded, w_qkv.reshape(w_qkv.shape[0], 3 * local_width), preferred_element_type=jnp.float32
    )
    projected = projected.reshape(row_count, 3, local_width)
    query_raw = projected[:, 0]
    key_raw = projected[:, 1]
    values = projected[:, 2].astype(jnp.bfloat16)
    query_sq, key_sq = lax.psum(
        (jnp.sum(query_raw * query_raw, axis=1), jnp.sum(key_raw * key_raw, axis=1)), "head"
    )
    queries = (query_raw * lax.rsqrt(query_sq / D + 1e-06)[:, None] * q_gain).astype(jnp.bfloat16)
    key_normed = (key_raw * lax.rsqrt(key_sq / D + 1e-06)[:, None] * k_gain).astype(jnp.bfloat16)
    head_count = local_width // DH
    query_heads = queries.reshape(row_count, head_count, DH)
    start_state = (
        jnp.full((head_count, row_count), -1e30, jnp.float32),
        jnp.zeros((head_count, row_count), jnp.float32),
        jnp.zeros((head_count, row_count, DH), jnp.float32),
    )
    all_rows = jnp.ones((row_count,), dtype=bool)
    carried = attend(start_state, query_heads, key_normed, values, all_rows)
    stacked = jnp.stack((key_normed, values))

    def pass_step(turn, loop_state):
        pieces, state_now = loop_state
        pieces = passed_along(pieces, "queue", 1)
        key_slab = jnp.mod(my_slab - turn, slabs)
        key_pos = jnp.mod(key_slab // 2 - offset[0], frames)

        def use_piece(state_in):
            return attend(state_in, query_heads, pieces[0], pieces[1], all_rows)

        def keep_state(state_in):
            return state_in

        state_now = lax.cond(key_pos <= position, use_piece, keep_state, state_now)
        return (pieces, state_now)

    stacked, carried = lax.fori_loop(1, slabs, pass_step, (stacked, carried))
    run_max, run_total, running = carried
    attn = (
        jnp.transpose(running / run_total[:, :, None], (1, 0, 2))
        .reshape(row_count, local_width)
        .astype(jnp.bfloat16)
    )
    partial_out = jnp.dot(attn, w_out, preferred_element_type=jnp.float32)
    proj = lax.psum_scatter(
        partial_out.astype(jnp.bfloat16), "head", scatter_dimension=1, tiled=True
    ).astype(jnp.float32)
    feature_start = lax.axis_index("head") * local_width
    gate_local = lax.dynamic_slice_in_dim(modulation[2], feature_start, local_width)
    updated = (latents.astype(jnp.float32) + gate_local * proj).astype(jnp.bfloat16)
    moved = passed_along(updated, "queue", -2)
    entry_slot = jnp.mod(offset[0] - 1, frames)
    fresh_half = lax.dynamic_slice_in_dim(fresh_frame, my_slab % 2 * row_count, row_count, 0)
    return jnp.where(my_frame == entry_slot, fresh_half, moved)


MESH = pl.DeviceIdType.MESH
ZS = 4
ROWS = 192
WIDTH = 384
HEADS_DEV = 3
PIECES = 2
VMEM_BYTES = 64 * 1024 * 1024 - 128 * 1024
PIECE = ROWS // PIECES


def arrived(buffer, sem):
    pltpu.make_async_copy(buffer, buffer, sem).wait()


def block_kernel(
    offset_ref, noise_hbm, lat_hbm, q_gain_hbm, k_gain_hbm, w_hbm, wout_hbm, mod_hbm, out_ref,
    noise_ref, lat_ref, q_gain, k_gain,
    w_v, wo_v, mod_v, lat_buf, mod_act, raw, stat_buf, stage, q_buf, k_buf, v_buf,
    o_buf, a_buf, w_col, s_buf, lat_next,
    load_sem, lat_send, lat_recv, st_send, st_recv, qkv_send, q_recv, k_recv, v_recv,
    f_send, o_send, o_recv, a_send, w_send, w_recv, mv_send, mv_recv,
):
    queue = lax.axis_index("queue")
    head = lax.axis_index("head")
    z, y = queue // 2, queue % 2
    x, c = head // 2, head % 2
    sib = x * 2 + (1 - c)
    xnb = (1 - x) * 2 + c
    diag = (1 - x) * 2 + (1 - c)
    peers = (head, sib, xnb, diag)
    below = queue - 2 + jnp.where(z == 0, 2 * ZS, 0)
    above = queue + 2 - jnp.where(z == ZS - 1, 2 * ZS, 0)
    swap_head = x * 2 + y
    on_diagonal = y == c

    def is_self(zt):
        return jnp.logical_and(on_diagonal, zt == z)

    loads = [
        pltpu.make_async_copy(mod_hbm, mod_v, load_sem.at[0]),
        pltpu.make_async_copy(w_hbm, w_v, load_sem.at[1]),
        pltpu.make_async_copy(wout_hbm, wo_v, load_sem.at[2]),
        pltpu.make_async_copy(lat_hbm, lat_ref, load_sem.at[3]),
        pltpu.make_async_copy(noise_hbm, noise_ref, load_sem.at[4]),
        pltpu.make_async_copy(q_gain_hbm, q_gain, load_sem.at[5]),
        pltpu.make_async_copy(k_gain_hbm, k_gain, load_sem.at[6]),
    ]
    for load in loads:
        load.start()

    barrier = pltpu.get_barrier_semaphore()

    def greet(q_id, h_id):
        pl.semaphore_signal(barrier, inc=1, device_id=(q_id, h_id), device_id_type=MESH)

    for peer in peers[1:]:
        greet(queue, peer)
    greet(below, head)
    greet(above, head)
    for zt in range(ZS):
        pl.when(jnp.logical_not(is_self(zt)))(lambda zt=zt: greet(zt * 2 + c, swap_head))
    pl.semaphore_wait(barrier, 5 + ZS - jnp.where(on_diagonal, 1, 0))

    def remote(src, dst, s_sem, r_sem, q_id, h_id):
        return pltpu.make_async_remote_copy(
            src_ref=src, dst_ref=dst, send_sem=s_sem, recv_sem=r_sem,
            device_id=(q_id, h_id), device_id_type=MESH,
        )

    loads[3].wait()
    pieces = [pl.ds(p * PIECE, PIECE) for p in range(PIECES)]
    to_x, forward = [], []
    for p, rows in enumerate(pieces):
        to_x.append(remote(
            lat_ref.at[rows], lat_buf.at[2, rows], lat_send.at[0, p], lat_recv.at[2, p], queue, xnb
        ))
        to_x[p].start()
        forward.append(remote(
            lat_buf.at[2, rows], lat_buf.at[3, rows], lat_send.at[2, p], lat_recv.at[3, p], queue, sib
        ))
    to_sib = remote(lat_ref, lat_buf.at[1], lat_send.at[1, 0], lat_recv.at[1, 0], queue, sib)
    to_sib.start()
    lat_move = remote(lat_ref, lat_next, mv_send, mv_recv, below, head)
    lat_move.start()
    for p, rows in enumerate(pieces):
        arrived(lat_buf.at[2, rows], lat_recv.at[2, p])
        forward[p].start()
    arrived(lat_buf.at[1], lat_recv.at[1, 0])
    loads[0].wait()
    for load in loads[4:]:
        load.wait()

    offset = lax.rem(offset_ref[0], ZS)

    def position_of(frame):
        return lax.rem(frame + ZS - offset, ZS)

    level = noise_ref[position_of(z)]
    for p, rows in enumerate(pieces):
        arrived(lat_buf.at[3, rows], lat_recv.at[3, p])

    def block(r):
        return (lat_ref[...] if r == 0 else lat_buf[r]).astype(jnp.float32)

    def columns(r):
        return pl.ds(pl.multiple_of(peers[r] * WIDTH, WIDTH), WIDTH)

    loads[2].wait()
    weights = []

    def send_weights(r, part):
        rows = pl.ds(part * (WIDTH // 2), WIDTH // 2)
        copy = remote(
            wo_v.at[rows, columns(r)], w_col.at[r, rows], w_send.at[r, part], w_recv.at[r, part], queue, peers[r]
        )
        copy.start()
        weights.append(copy)

    mean = sum(jnp.sum(block(r), axis=1, keepdims=True) for r in range(4)) / D
    square = jnp.zeros((ROWS, 1), jnp.float32)
    for r in range(4):
        centered = block(r) - mean
        square += jnp.sum(centered * centered, axis=1, keepdims=True)
    inv = lax.rsqrt(square / D + 1e-06)
    for r in range(4):
        shift = mod_v[0, pl.ds(level, 1), columns(r)]
        scale = mod_v[1, pl.ds(level, 1), columns(r)]
        normed = (block(r) - mean) * inv
        mod_act[:, columns(r)] = (normed * (1.0 + scale) + shift).astype(jnp.bfloat16)

    loads[1].wait()
    sends = []

    def send_part(part, buf, recv_sem):
        for j in range(HEADS_DEV):
            zt = j + c
            mine = is_self(zt)
            src = stage.at[part, j]
            dst = buf.at[z] if part == 0 else buf.at[0, z]
            far = remote(src, dst, qkv_send.at[part, j], recv_sem.at[z], zt * 2 + c, swap_head)
            near = pltpu.make_async_copy(src, dst, recv_sem.at[z])
            pl.when(mine)(near.start)
            pl.when(jnp.logical_not(mine))(far.start)
            sends.append((mine, far))

    values = jnp.dot(mod_act[...], w_v[2], preferred_element_type=jnp.float32)
    for j in range(HEADS_DEV):
        stage[2, j] = values[:, j * DH:(j + 1) * DH].astype(jnp.bfloat16)
    send_part(2, v_buf, v_recv)

    sums = []
    for i in range(2):
        projected = jnp.dot(mod_act[...], w_v[i], preferred_element_type=jnp.float32)
        raw[i] = projected
        sums.append(jnp.sum(projected * projected, axis=1, keepdims=True))
    lane = lax.broadcasted_iota(jnp.int32, (256, 128), 1)
    padding = jnp.zeros((256 - ROWS, 1), jnp.float32)
    spread = jnp.where(
        lane == 0,
        jnp.concatenate([sums[0], padding], axis=0),
        jnp.concatenate([sums[1], padding], axis=0),
    )
    stat_buf[0] = jnp.transpose(spread)[:8]
    stats = [
        remote(stat_buf.at[0], stat_buf.at[r], st_send.at[r], st_recv.at[r], queue, peers[r])
        for r in (2, 3, 1)
    ]
    for copy in stats:
        copy.start()

    for r in (1, 2, 3):
        arrived(stat_buf.at[r], st_recv.at[r])
    total_sq = stat_buf[0] + stat_buf[1] + stat_buf[2] + stat_buf[3]
    rates = lax.rsqrt(total_sq / D + 1e-06)
    rates = jnp.transpose(jnp.concatenate([rates] * 16, axis=0))[:ROWS]
    for part, buf, recv_sem in ((1, k_buf, k_recv), (0, q_buf, q_recv)):
        rate = rates[:, part:part + 1]
        gain = (q_gain, k_gain)[part][...].reshape(1, WIDTH)
        for j in range(HEADS_DEV):
            cols = slice(j * DH, (j + 1) * DH)
            stage[part, j] = (raw[part, :, cols] * rate * gain[:, cols]).astype(jnp.bfloat16)
        send_part(part, buf, recv_sem)

    for r in (3, 2, 1):
        for part in range(2):
            send_weights(r, part)

    active = jnp.logical_and(z - y >= 0, z - y <= 2)
    slot = jnp.where(active, z - y, 0)

    @pl.when(active)
    def _():
        forwards = []
        for kind, (buf, recv_sem) in enumerate(((v_buf, v_recv), (k_buf, k_recv))):
            for s in range(ZS):
                arrived(buf.at[0, s], recv_sem.at[s])
                copy = remote(
                    buf.at[0, s], buf.at[1, s], f_send.at[kind, s], recv_sem.at[ZS + s], queue, sib
                )
                copy.start()
                forwards.append(copy)
        for buf, recv_sem in ((v_buf, v_recv), (k_buf, k_recv)):
            for s in range(ZS):
                arrived(buf.at[1, s], recv_sem.at[ZS + s])
        keys = k_buf[...].reshape(2 * ZS * ROWS, DH)
        vals = v_buf[...].reshape(2 * ZS * ROWS, DH)
        column = lax.broadcasted_iota(jnp.int32, (1, 2 * ZS * ROWS), 1)
        frame = jnp.zeros_like(column)
        for t in range(1, 2 * ZS):
            frame += jnp.where(column >= t * ROWS, 1 if t != ZS else 1 - ZS, 0)
        key_pos = frame - offset
        key_pos = jnp.where(key_pos < 0, key_pos + ZS, key_pos)
        order = (z, z + 1 - 2 * (z % 2), (z + 2) % ZS, ZS - 1 - z)

        def score_into(i):
            arrived(q_buf.at[order[i]], q_recv.at[order[i]])
            s_buf[i % 2] = lax.dot_general(
                q_buf[order[i]], keys, (((1,), (1,)), ((), ())), preferred_element_type=jnp.float32
            )

        outs = []
        score_into(0)
        for i, s in enumerate(order):
            if i + 1 < ZS:
                score_into(i + 1)
            bias = jnp.where(key_pos <= position_of(s), 0.0, -1e30)
            scores = s_buf[i % 2] * (DH ** (-0.5) * math.log2(math.e)) + bias
            top = jnp.max(scores, axis=1, keepdims=True)
            e = jnp.exp2(scores - top)
            total = jnp.sum(e, axis=1, keepdims=True)
            added = jnp.dot(e.astype(jnp.bfloat16), vals, preferred_element_type=jnp.float32)
            o_buf[i] = (added / total).astype(jnp.bfloat16)
            zt = (s + ZS - 1) % ZS
            mine = is_self(zt)
            far = remote(
                o_buf.at[i], a_buf.at[0, slot], o_send.at[0, i], o_recv.at[0, slot], zt * 2 + c, swap_head
            )
            near = pltpu.make_async_copy(o_buf.at[i], a_buf.at[0, slot], o_recv.at[0, slot])
            pl.when(mine)(near.start)
            pl.when(jnp.logical_not(mine))(far.start)
            outs.append((mine, far))
        for copy in forwards:
            copy.wait_send()
        for mine, far in outs:
            pl.when(jnp.logical_not(mine))(far.wait_send)

    shared = []

    def share(r, to, j, target):
        copy = remote(
            a_buf.at[r, j], a_buf.at[to, j], a_send.at[to, j], o_recv.at[to, j], queue, target
        )
        copy.start()
        shared.append(copy)

    for j in range(HEADS_DEV):
        arrived(a_buf.at[0, j], o_recv.at[0, j])
        share(0, 2, j, xnb)
        share(0, 1, j, sib)

    def out_block(r):
        attn = jnp.concatenate([a_buf[r, j] for j in range(HEADS_DEV)], axis=1)
        own = wo_v[:, columns(0)] if r == 0 else w_col[r]
        return jnp.dot(attn, own, preferred_element_type=jnp.float32)

    proj = out_block(0)
    for j in range(HEADS_DEV):
        arrived(a_buf.at[2, j], o_recv.at[2, j])
        share(2, 3, j, sib)
    for r in (1, 2, 3):
        for part in range(2):
            rows = pl.ds(part * (WIDTH // 2), WIDTH // 2)
            arrived(w_col.at[r, rows], w_recv.at[r, part])
    proj += out_block(2)
    gate = mod_v[2, pl.ds(noise_ref[position_of((z + 1) % ZS)], 1), columns(0)]
    arrived(lat_next, mv_recv)
    for r in (1, 3):
        for j in range(HEADS_DEV):
            arrived(a_buf.at[r, j], o_recv.at[r, j])
        proj += out_block(r)
    out_ref[...] = (lat_next[...].astype(jnp.float32) + gate * proj).astype(jnp.bfloat16)
    for copy in (*to_x, to_sib, *forward, *stats, *weights, *shared, lat_move):
        copy.wait_send()
    for mine, far in sends:
        pl.when(jnp.logical_not(mine))(far.wait_send)


def local_fused(latents, fresh_frame, noise_level, offset, mod_table, w_qkv, w_out, q_gain, k_gain):
    bf16, f32 = jnp.bfloat16, jnp.float32
    dma = pltpu.SemaphoreType.DMA
    vmem = pl.BlockSpec(memory_space=pltpu.VMEM)
    hbm = pl.BlockSpec(memory_space=pl.ANY)
    moved = pl.pallas_call(
        block_kernel,
        out_shape=jax.ShapeDtypeStruct((ROWS, WIDTH), bf16),
        in_specs=[pl.BlockSpec(memory_space=pltpu.SMEM)] + [hbm] * 7,
        out_specs=vmem,
        scratch_shapes=[
            pltpu.SMEM(noise_level.shape, jnp.int32),
            pltpu.VMEM((ROWS, WIDTH), bf16),
            pltpu.VMEM((WIDTH,), f32),
            pltpu.VMEM((WIDTH,), f32),
            pltpu.VMEM((3, D, WIDTH), bf16),
            pltpu.VMEM((WIDTH, D), bf16),
            pltpu.VMEM((3, mod_table.shape[0], D), f32),
            pltpu.VMEM((4, ROWS, WIDTH), bf16),
            pltpu.VMEM((ROWS, D), bf16),
            pltpu.VMEM((2, ROWS, WIDTH), f32),
            pltpu.VMEM((4, 8, 256), f32),
            pltpu.VMEM((3, HEADS_DEV, ROWS, DH), bf16),
            pltpu.VMEM((ZS, ROWS, DH), bf16),
            pltpu.VMEM((2, ZS, ROWS, DH), bf16),
            pltpu.VMEM((2, ZS, ROWS, DH), bf16),
            pltpu.VMEM((ZS, ROWS, DH), bf16),
            pltpu.VMEM((4, HEADS_DEV, ROWS, DH), bf16),
            pltpu.VMEM((4, WIDTH, WIDTH), bf16),
            pltpu.VMEM((2, ROWS, 2 * ZS * ROWS), f32),
            pltpu.VMEM((ROWS, WIDTH), bf16),
            dma((7,)),
            dma((3, PIECES)),
            dma((4, PIECES)),
            dma((4,)),
            dma((4,)),
            dma((3, HEADS_DEV)),
            dma((ZS,)),
            dma((2 * ZS,)),
            dma((2 * ZS,)),
            dma((2, ZS)),
            dma((1, ZS)),
            dma((4, HEADS_DEV)),
            dma((4, HEADS_DEV)),
            dma((4, 2)),
            dma((4, 2)),
            dma,
            dma,
        ],
        compiler_params=pltpu.CompilerParams(
            collective_id=0, has_side_effects=True, vmem_limit_bytes=VMEM_BYTES
        ),
    )(
        offset,
        noise_level,
        latents,
        q_gain,
        k_gain,
        jnp.transpose(w_qkv, (1, 0, 2)),
        w_out,
        jnp.transpose(mod_table, (1, 0, 2)),
    )
    my_slab = lax.axis_index("queue")
    entry_slot = jnp.mod(offset[0] - 1, ZS)
    fresh_half = lax.dynamic_slice_in_dim(fresh_frame, my_slab % 2 * ROWS, ROWS, 0)
    return jnp.where(my_slab // 2 == entry_slot, fresh_half, moved)


def solution(mesh):
    fits = mesh.shape["queue"] == 2 * ZS and mesh.shape["head"] == 4
    return jax.shard_map(
        local_fused if fits else local,
        mesh=mesh,
        in_specs=(
            P("queue", "head"),
            P(None, "head"),
            P(),
            P(),
            P(),
            P(None, None, "head"),
            P("head", None),
            P("head"),
            P("head"),
        ),
        out_specs=P("queue", "head"),
        check_vma=False,
    )
```
